32 devices in a mesh: dp: 8 (over y, x, core), expert: 4 (over z).
Axes of the slice: x: 2, y: 2, z: 4, core: 2. Of those that a mesh axis runs over, the one named last changes fastest.
Arguments:
- tokens: bfloat16 [2048, 2048], P('expert', 'dp'), may hold values from -6 to 6
- routes: int32 [2048, 2], P('expert'), may hold values from 0 to 3, all different within a row; in each aligned block of 512 rows (0 to 511, 512 to 1023, ...) at most 384 rows name the same one
- scores: int32 [2048, 2], P('expert'), may hold values from 1 to 1023
- gate_weight: bfloat16 [4, 2048, 8192], P('expert', None, 'dp'), may hold values from -0.125 to 0.125
- up_weight: bfloat16 [4, 2048, 8192], P('expert', None, 'dp'), may hold values from -0.125 to 0.125
- down_weight: bfloat16 [4, 8192, 2048], P('expert', 'dp'), may hold values from -0.0625 to 0.0625
Outputs:
- layer_out: bfloat16 [2048, 2048], P('expert', 'dp')
The draws below stay inside these ranges and needn't reach their ends.
Inputs may be any that keep to these rules, and one draw needn't show every extreme that they name: `routes`: each row names 2 different experts. Within each aligned block of 512 rows no expert is named by more than 384 rows, and in every draw some expert is named by exactly 384 rows of a block.
All inputs are finite; a program needn't handle non-finite values.
Results may differ from the reference program's by a relative error of at most 0.025.
Values may be sent and summed in bfloat16 or wider, within the bound.
No kernel may reach another device: no remote copies, remote signals or barrier semaphores. Data moves between devices by JAX's collectives and lax.ppermute only.
A program may use at most 64 MiB of HBM per device.

```python
import math
import jax
import jax.numpy as jnp
import numpy as np
from jax import lax

D = 2048
FF = 8192
TOP = 2
TOK_E = 512
EXPERTS = 4
CAP = 384
TOKENS = 2048
N_DP = 8
N_EXPERT = 4


def place_ends(values, stream_key, smallest, largest):
    extent = values.shape
    index_at = [jax.random.randint(jax.random.fold_in(stream_key, axis), (), 0, extent[axis]) for axis in range(len(extent))]
    values = values.at[tuple(index_at)].set(smallest)
    longest = extent.index(max(extent))
    index_at[longest] = (index_at[longest] + 1) % extent[longest]
    return values.at[tuple(index_at)].set(largest)


def level_of(key, shape, pieces, least, largest):
    gain, own = 1.0, jax.random.fold_in(key, 6)
    for axis_at, parts in pieces:
        heights = jnp.exp(jax.random.uniform(jax.random.fold_in(own, axis_at), (parts,), jnp.float32, least / len(pieces), largest / len(pieces)))
        gain = gain * jnp.repeat(heights, shape[axis_at] // parts).reshape([-1 if axis == axis_at else 1 for axis in range(len(shape))])
    return gain


def routed_block(stream_key, own, number, rows, amount, top, bound, lean):
    sequence = jax.random.permutation(stream_key, amount)
    crowded, common = shares(amount, rows * top, bound, lean, True), shares(amount, rows * top, bound, lean, False)
    places = jnp.arange(amount)

    def named(sizes, offset_by):
        used = int((sizes > 0).sum())
        fixed = max(1, used // 4)
        shifted = fixed + (places - fixed + offset_by * (used - fixed)) % max(1, amount - fixed)
        return jnp.zeros((amount,), jnp.int32).at[sequence[jnp.where(places < fixed, places, shifted)]].set(jnp.asarray(sizes, jnp.int32))

    sizes = jnp.where(number % 4 == 0, named(crowded, number // 4), named(common, number - number // 4 - 1))
    mixed = jax.random.permutation(jax.random.fold_in(own, 3), amount)
    donor, receiver = mixed[0:amount // 2 * 2:2], mixed[1:amount // 2 * 2:2]
    margin = jnp.minimum(sizes[donor] - 1, bound - sizes[receiver]) // 2
    margin = jnp.where((donor == sequence[0]) | (receiver == sequence[0]) | (sizes[receiver] == 0), 0, jnp.maximum(margin, 0))
    shifted = jax.random.randint(jax.random.fold_in(own, 4), (amount // 2,), 0, 1 << 20) % (margin + 1)
    sizes = sizes.at[donor].add(-shifted).at[receiver].add(shifted)
    items = jnp.searchsorted(jnp.cumsum(sizes), jnp.arange(rows * top), side="right").astype(jnp.int32)
    grid = items.reshape(top, rows).T
    grid = grid[jax.random.permutation(jax.random.fold_in(own, 1), rows)]
    offset_by = jax.random.randint(jax.random.fold_in(own, 2), (rows, 1), 0, top)
    return jnp.take_along_axis(grid, (jnp.arange(top)[None, :] + offset_by) % top, axis=1)


def shares(number_of, total, most, skew, full):
    loads = [(1 << 20) // math.isqrt(grade ** skew) + 1 for grade in range(1, number_of + 1)]
    largest = most if full else min(most, max(-(-total // number_of), total * loads[0] // sum(loads)))
    least = 1 if total - largest >= number_of - 1 else 0
    holding, surplus = [largest] + [least] * (number_of - 1), total - largest - least * (number_of - 1)
    while surplus > 0:
        candidates = [i for i in range(1, number_of) if holding[i] < largest] or [i for i in range(1, number_of) if holding[i] < most]
        pool, left = sum([loads[i] for i in candidates]), surplus
        for i in candidates:
            more = min(most - holding[i], max(1, left * loads[i] // pool), surplus)
            holding[i] = holding[i] + more
            surplus = surplus - more
    return np.array(holding)


def noise(key, dims, scale, bound, cuts=(), kind=jnp.bfloat16):
    gain = level_of(key, dims, cuts, -0.22, 0.18) if cuts else 1.0
    result = jax.random.normal(key, dims, jnp.float32) * scale * gain
    return jnp.minimum(jnp.maximum(result, -bound), bound).astype(kind)


def setup_inputs(seed: int = 0) -> dict:
    seeds = jax.random.split(jax.random.key(seed), 7)
    tokens = noise(seeds[0], (TOKENS, D), 1.0, 6.0, ((0, 4), (1, 8)))
    routes_keys = jax.random.split(jax.random.fold_in(seeds[1], 1), TOKENS // TOK_E)
    routes_turns = jax.random.permutation(jax.random.fold_in(seeds[1], 3), TOKENS // TOK_E)
    routes = jax.vmap(lambda own, number: routed_block(jax.random.fold_in(seeds[1], 2), own, number, TOK_E, EXPERTS, TOP, CAP, 2))(routes_keys, routes_turns).reshape((TOKENS, TOP))
    scores = place_ends(jax.random.randint(seeds[2], (TOKENS, TOP), 1, 1024), jax.random.fold_in(seeds[2], 1), 1, 1023).astype(jnp.int32)
    gate_weight = noise(seeds[3], (EXPERTS, D, FF), D ** -0.5, 0.125, ((0, 4), (2, 8)))
    up_weight = noise(seeds[4], (EXPERTS, D, FF), D ** -0.5, 0.125, ((0, 4), (2, 8)))
    down_weight = noise(seeds[5], (EXPERTS, FF, D), FF ** -0.5, 0.0625, ((0, 4), (1, 8)))
    return {"tokens": tokens, "routes": routes, "scores": scores, "gate_weight": gate_weight, "up_weight": up_weight, "down_weight": down_weight}


def reference(tokens, routes, scores, gate_weight, up_weight, down_weight):
    row_count = tokens.shape[0]
    expert_count = gate_weight.shape[0]
    slot_count = N_EXPERT * CAP
    block_cols = FF // N_DP
    flat_routes = routes.reshape(-1)
    onehot = (flat_routes[:, None] == jnp.arange(expert_count, dtype=jnp.int32)[None, :]).astype(jnp.int32)
    earlier = jnp.cumsum(onehot, axis=0) - onehot
    slot_rank = jnp.sum(onehot * earlier, axis=1).astype(jnp.int32)
    row_ids = jnp.repeat(jnp.arange(row_count, dtype=jnp.int32), TOP)
    row_table = jnp.zeros((expert_count, slot_count), jnp.int32).at[flat_routes, slot_rank].set(row_ids)

    def expert_result(packed):
        row_index, gate_mat, up_mat, down_mat = packed
        gathered = tokens[row_index]
        gate = jnp.dot(gathered, gate_mat, preferred_element_type=jnp.float32)
        upval = jnp.dot(gathered, up_mat, preferred_element_type=jnp.float32)
        hidden = (jax.nn.silu(gate) * upval).astype(jnp.bfloat16)

        def add_block(block, total):
            start = (block * block_cols).astype(jnp.int32)
            hidden_block = lax.dynamic_slice_in_dim(hidden, start, block_cols, 1)
            down_block = lax.dynamic_slice_in_dim(down_mat, start, block_cols, 0)
            rounded = lax.optimization_barrier(jnp.dot(hidden_block, down_block, preferred_element_type=jnp.float32).astype(jnp.bfloat16))
            return total + rounded.astype(jnp.float32)

        return lax.fori_loop(0, N_DP, add_block, jnp.zeros((slot_count, D), jnp.float32))

    results = lax.map(expert_result, (row_table, gate_weight, up_weight, down_weight))
    picked = results[flat_routes, slot_rank].reshape(row_count, TOP, D)
    weight = scores.astype(jnp.float32)
    weight = weight / jnp.sum(weight, axis=1, keepdims=True)
    combined = jnp.sum(weight[:, :, None] * picked, axis=1)
    return combined.astype(jnp.bfloat16)
```

```python
import functools

import jax
import jax.numpy as jnp
from jax import lax
from jax.experimental import pallas as pl
from jax.experimental.pallas import tpu as pltpu
from jax.sharding import PartitionSpec as P

F32 = jnp.float32
BF16 = jnp.bfloat16
ANY = pl.BlockSpec(memory_space=pl.ANY)
VMEM = pl.BlockSpec(memory_space=pltpu.VMEM)
SMEM = pl.BlockSpec(memory_space=pltpu.SMEM)
ORDER = (0, 1, 2, 3)
CORE = 1


def first_link(core):
    return 2 + 2 * core


def second_link(core):
    return 4 - 2 * core


def over_core(value):
    return lax.ppermute(value, "dp", [(i, i ^ CORE) for i in range(lax.axis_size("dp"))])


def over_first(value):
    return lax.ppermute(value, "dp", [(i, i ^ first_link(i & 1)) for i in range(lax.axis_size("dp"))])


def over_second(value):
    return lax.ppermute(value, "dp", [(i, i ^ second_link(i & 1)) for i in range(lax.axis_size("dp"))])


def over_expert(value, mask):
    return lax.ppermute(value, "expert", [(i, i ^ mask) for i in range(lax.axis_size("expert"))])


def ordered(body, operand_count, dep_count):
    def kernel(*refs):
        body(*refs[:operand_count], *refs[operand_count + dep_count :])

    return kernel


def call(body, name, shapes, operands, deps=(), specs=None, scratch=(), vmem=16):
    return pl.pallas_call(
        ordered(body, len(operands), len(deps)),
        out_shape=[jax.ShapeDtypeStruct(s, BF16) for s in shapes],
        in_specs=(specs or [VMEM] * len(operands)) + [ANY] * len(deps),
        out_specs=[VMEM] * len(shapes),
        scratch_shapes=list(scratch),
        compiler_params=pltpu.CompilerParams(vmem_limit_bytes=vmem << 20),
        cost_estimate=pl.CostEstimate(flops=0, bytes_accessed=0, transcendentals=0),
        name=name,
    )(*operands, *deps)


def slots_of(routes_ref, expert_count):
    row_count = routes_ref.shape[1]
    first, second = routes_ref[0:1, :], routes_ref[1:2, :]
    ids = lax.broadcasted_iota(jnp.int32, (8 * pl.cdiv(expert_count, 8), row_count), 0)
    named = (first == ids) | (second == ids)
    above = lax.broadcasted_iota(jnp.int32, (row_count, row_count), 0)
    below = lax.broadcasted_iota(jnp.int32, (row_count, row_count), 1)
    strict = (above < below).astype(F32).astype(BF16)
    earlier = jnp.dot(named.astype(F32).astype(BF16), strict, preferred_element_type=F32)
    return jnp.where(named, earlier.astype(jnp.int32), -1), ids


def dispatch_kernel(me_ref, routes_ref, tokens_ref, *out_refs):
    capacity = out_refs[0].shape[0]
    slots, ids = slots_of(routes_ref, len(out_refs))
    tokens = tokens_ref[...]
    slot_ids = lax.broadcasted_iota(jnp.int32, (capacity, tokens.shape[0]), 0)
    for j in range(len(out_refs)):
        mine = jnp.max(jnp.where(ids == me_ref[0] ^ j, slots, -1), axis=0, keepdims=True)
        placement = (slot_ids == mine).astype(F32).astype(BF16)
        out_refs[j][...] = jnp.dot(placement, tokens, preferred_element_type=F32).astype(BF16)


def mixing_kernel(me_ref, routes_ref, scores_ref, *out_refs):
    row_count, capacity = out_refs[0].shape
    slots, ids = slots_of(routes_ref, len(out_refs))
    scores = scores_ref[...].astype(F32)
    weights = scores / jnp.sum(scores, axis=0, keepdims=True)
    slot_ids = lax.broadcasted_iota(jnp.int32, (capacity, row_count), 0)
    for j in range(len(out_refs)):
        expert = me_ref[0] ^ j
        mine = jnp.max(jnp.where(ids == expert, slots, -1), axis=0, keepdims=True)
        weight = jnp.where(routes_ref[0:1, :] == expert, weights[0:1, :], weights[1:2, :])
        out_refs[j][...] = jnp.where(slot_ids == mine, weight, 0.0).T.astype(BF16)


def mixing(me, routes, scores, expert_count, capacity, deps=()):
    return call(
        mixing_kernel,
        "mixing",
        [(routes.shape[0], capacity)] * expert_count,
        [me, routes.T, scores.T],
        deps,
        specs=[SMEM, VMEM, VMEM],
    )


def combine_kernel(*refs):
    count = (len(refs) - 1) // 2
    total = None
    for mix_ref, rows_ref in zip(refs[:count], refs[count : 2 * count]):
        part = jnp.dot(mix_ref[...], rows_ref[...], preferred_element_type=F32)
        total = part if total is None else total + part
    refs[-1][...] = total.astype(BF16)


def stack_kernel(low_ref, high_ref, out_ref):
    out_ref[0] = low_ref[...]
    out_ref[1] = high_ref[...]


def pick_kernel(pair_ref, out_ref):
    out_ref[...] = pair_ref[0]


def expert_kernel(
    me_ref, pair_ref, near_ref, far_ref, diag_ref, other_diag_ref, gate_ref, up_ref, down_ref,
    own_ref, keep_ref, give_ref, hidden,
):
    me = me_ref[1]
    core = me & 1
    mine, theirs = first_link(core), second_link(core)
    width = pair_ref.shape[2]
    units = hidden.shape[1]
    tile = 256
    pieces = (
        (pair_ref.at[0], me),
        (pair_ref.at[1], me ^ 1),
        (near_ref.at[0], me ^ mine),
        (near_ref.at[1], me ^ mine ^ 1),
        (far_ref.at[1], me ^ theirs),
        (far_ref.at[0], me ^ theirs ^ 1),
        (diag_ref, me ^ 6),
        (other_diag_ref, me ^ 7),
    )
    for start in range(0, units, tile):
        gate = up = None
        for ref, source in pieces:
            rows = pl.ds(pl.multiple_of(source * width, width), width)
            x = ref[...]
            g = jnp.dot(x, gate_ref[rows, start : start + tile], preferred_element_type=F32)
            u = jnp.dot(x, up_ref[rows, start : start + tile], preferred_element_type=F32)
            gate = g if gate is None else gate + g
            up = u if up is None else up + u
        hidden[:, start : start + tile] = (gate / (1.0 + jnp.exp(-gate)) * up).astype(BF16)
    results = (
        (keep_ref.at[2], me ^ 6),
        (give_ref.at[2], me ^ 7),
        (give_ref.at[1], me ^ theirs),
        (give_ref.at[0], me ^ theirs ^ 1),
        (keep_ref.at[0], me ^ mine),
        (keep_ref.at[1], me ^ mine ^ 1),
        (own_ref.at[0], me),
        (own_ref.at[1], me ^ 1),
    )
    for ref, target in results:
        columns = pl.ds(pl.multiple_of(target * width, width), width)
        ref[...] = jnp.dot(hidden[...], down_ref[:, columns], preferred_element_type=F32).astype(BF16)


def diag_sum_kernel(keep_ref, got_ref, out_ref):
    out_ref[...] = (keep_ref[2].astype(F32) + got_ref[2].astype(F32)).astype(BF16)


def near_sum_kernel(keep_ref, got_ref, relayed_ref, out_ref):
    out_ref[0] = (keep_ref[0].astype(F32) + got_ref[0].astype(F32) + relayed_ref[...].astype(F32)).astype(BF16)
    out_ref[1] = (keep_ref[1].astype(F32) + got_ref[1].astype(F32)).astype(BF16)


def other_sum_kernel(own_ref, near_ref, out_ref):
    out_ref[...] = (own_ref[1].astype(F32) + near_ref[1].astype(F32)).astype(BF16)


def last_sum_kernel(own_ref, near_ref, other_ref, out_ref):
    out_ref[...] = (own_ref[0].astype(F32) + near_ref[0].astype(F32) + other_ref[...].astype(F32)).astype(BF16)


def copy_kernel(in_ref, out_ref):
    out_ref[...] = in_ref[...]


def load_kernel(gate_ref, up_ref, down_ref, new_gate_ref, new_up_ref, new_down_ref, sems):
    pairs = ((gate_ref, new_gate_ref), (up_ref, new_up_ref), (down_ref, new_down_ref))
    copies = [pltpu.make_async_copy(old, new, sems.at[i]) for i, (old, new) in enumerate(pairs)]
    for copy in copies:
        copy.start()
    for copy in copies:
        copy.wait()


def experts_by_chips(outgoing, weights, expert_count, capacity, me, routes, scores):
    width = outgoing[0].shape[1]
    units = weights[0].shape[1]
    one, two, three = (capacity, width), (2, capacity, width), (3, capacity, width)
    n = expert_count
    pieces = [outgoing[0]] + [over_expert(outgoing[j], j) for j in range(1, n)]
    near, far, diag, picked, pair = {}, {}, {}, {}, {}
    own, keep, got, relayed, total, back = {}, {}, {}, {}, {}, {}
    summed, nearby = {}, {}

    def gather_start(j, *deps):
        piece = pieces[j]
        if j:
            piece = call(copy_kernel, "arrived", [one], [piece], deps)[0]
        pair[j] = call(stack_kernel, "pair", [two], [piece, over_core(piece)], deps)[0]
        near[j] = over_first(pair[j])

    def gather_relay(j, *deps):
        picked[j] = call(pick_kernel, "pick", [one], [near[j]], deps)[0]
        far[j] = over_core(near[j])
        diag[j] = over_second(picked[j])

    def compute(j, deps, late_deps):
        diag[j] = call(copy_kernel, "relayed", [one], [diag[j]], deps)[0]
        own[j], keep[j], give = call(
            expert_kernel,
            "expert",
            [two, three, three],
            [me, pair[j], near[j], far[j], diag[j], over_core(diag[j]), gate_mat, up_mat, down_mat],
            late_deps,
            specs=[SMEM] + [VMEM] * 8,
            scratch=[pltpu.VMEM((capacity, units), BF16)],
            vmem=16,
        )
        got[j] = over_core(give)

    def scatter_relay(j, *deps):
        summed[j] = call(diag_sum_kernel, "diag_sum", [one], [keep[j], got[j]], deps)[0]
        relayed[j] = over_second(summed[j])

    def scatter_near(j, *deps):
        nearby[j] = call(near_sum_kernel, "near_sum", [two], [keep[j], got[j], relayed[j]], deps)[0]
        total[j] = over_first(nearby[j])

    def scatter_end(j, *deps):
        other = over_core(call(other_sum_kernel, "other_sum", [one], [own[j], total[j]], deps)[0])
        result = call(last_sum_kernel, "last_sum", [one], [own[j], total[j], other])[0]
        back[j] = over_expert(result, j) if j else result

    c0, c1, c2, c3 = ORDER
    gather_start(c0)
    mix = mixing(me, routes, scores, n, capacity, (pair[c0],))
    gather_relay(c0, mix[0])
    gather_start(c1, picked[c0])
    gate_mat, up_mat, down_mat = call(
        load_kernel,
        "load",
        [w.shape for w in weights],
        [pltpu.with_memory_space_constraint(w, pltpu.HBM) for w in weights],
        (pair[c1],),
        specs=[ANY] * 3,
        scratch=[pltpu.SemaphoreType.DMA((3,))],
    )
    gather_relay(c1, gate_mat)
    gather_start(c2, picked[c1])
    compute(c0, (pair[c2],), ())
    gather_start(c3, own[c0])
    gather_relay(c2, pair[c3])
    compute(c1, (picked[c2],), ())
    gather_relay(c3, own[c1])
    scatter_relay(c0, picked[c3])
    compute(c2, (summed[c0],), ())
    scatter_near(c0, own[c2])
    scatter_relay(c1, nearby[c0])
    compute(c3, (summed[c1],), ())
    scatter_near(c1, own[c3])
    scatter_relay(c2, nearby[c1])
    scatter_end(c0, summed[c2])
    scatter_relay(c3, summed[c2])
    scatter_near(c2, summed[c3])
    scatter_end(c1, nearby[c2])
    scatter_near(c3, nearby[c2])
    scatter_end(c2, nearby[c3])
    scatter_end(c3, nearby[c3])
    return mix, [back[j] for j in range(n)]


def experts_by_axes(outgoing, weights):
    expert_count = lax.axis_size("expert")
    capacity, width = outgoing[0].shape
    me = lax.axis_index("expert")
    order = jnp.arange(expert_count) ^ me
    rows = jnp.stack(outgoing)[order]
    rows = lax.all_to_all(rows, "expert", split_axis=0, concat_axis=0, tiled=True)
    rows = lax.all_gather(rows.reshape(-1, width), "dp", axis=1, tiled=True)
    gate = jnp.dot(rows, weights[0], preferred_element_type=F32)
    up = jnp.dot(rows, weights[1], preferred_element_type=F32)
    hidden = (jax.nn.silu(gate) * up).astype(BF16)
    part = jnp.dot(hidden, weights[2], preferred_element_type=F32).astype(BF16)
    total = lax.psum_scatter(part, "dp", scatter_dimension=1, tiled=True)
    back = lax.all_to_all(
        total.reshape(expert_count, capacity, width), "expert", split_axis=0, concat_axis=0, tiled=True
    )[order]
    return [back[j] for j in range(expert_count)]


def shards(tokens, routes, scores, gate_weight, up_weight, down_weight):
    expert_count = lax.axis_size("expert")
    row_count = tokens.shape[0]
    capacity = 3 * row_count // expert_count
    me = jnp.stack([lax.axis_index("expert"), lax.axis_index("dp")]).astype(jnp.int32)
    weights = gate_weight[0], up_weight[0], down_weight[0]

    shape = (capacity, tokens.shape[1])
    outgoing = call(
        dispatch_kernel,
        "dispatch",
        [shape] * expert_count,
        [me, routes.T, tokens],
        specs=[SMEM, VMEM, VMEM],
    )
    if expert_count == 4 and lax.axis_size("dp") == 8:
        mix, results = experts_by_chips(outgoing, weights, expert_count, capacity, me, routes, scores)
    else:
        mix = mixing(me, routes, scores, expert_count, capacity)
        results = experts_by_axes(outgoing, weights)
    return call(combine_kernel, "combine", [tokens.shape], [*mix, *results])[0]


def solution(mesh):
    return jax.shard_map(
        shards,
        mesh=mesh,
        in_specs=(
            P("expert", "dp"),
            P("expert", None),
            P("expert", None),
            P("expert", None, "dp"),
            P("expert", None, "dp"),
            P("expert", "dp", None),
        ),
        out_specs=P("expert", "dp"),
        check_vma=False,
    )
```

```python
import functools

import jax
import jax.numpy as jnp
from jax import lax
from jax.experimental import pallas as pl
from jax.experimental.pallas import tpu as pltpu
from jax.sharding import PartitionSpec as P

F32 = jnp.float32
BF16 = jnp.bfloat16
ANY = pl.BlockSpec(memory_space=pl.ANY)
VMEM = pl.BlockSpec(memory_space=pltpu.VMEM)
SMEM = pl.BlockSpec(memory_space=pltpu.SMEM)
CORE, X, Y, DIAGONAL = 1, 2, 4, 6
ORDER = (0, 2, 3, 1)


def over_dp(value, mask):
    return lax.ppermute(value, "dp", [(i, i ^ mask) for i in range(lax.axis_size("dp"))])


def over_expert(value, mask):
    return lax.ppermute(value, "expert", [(i, i ^ mask) for i in range(lax.axis_size("expert"))])


def ordered(body, operand_count, dep_count):
    def kernel(*refs):
        body(*refs[:operand_count], *refs[operand_count + dep_count :])

    return kernel


def call(body, name, shapes, operands, deps=(), specs=None, scratch=(), vmem=16, dtype=BF16):
    return pl.pallas_call(
        ordered(body, len(operands), len(deps)),
        out_shape=[jax.ShapeDtypeStruct(s, dtype) for s in shapes],
        in_specs=(specs or [VMEM] * len(operands)) + [ANY] * len(deps),
        out_specs=[VMEM] * len(shapes),
        scratch_shapes=list(scratch),
        compiler_params=pltpu.CompilerParams(vmem_limit_bytes=vmem << 20),
        cost_estimate=pl.CostEstimate(flops=0, bytes_accessed=0, transcendentals=0),
        name=name,
    )(*operands, *deps)


def slots_of(routes_ref, expert_count):
    row_count = routes_ref.shape[1]
    first, second = routes_ref[0:1, :], routes_ref[1:2, :]
    ids = lax.broadcasted_iota(jnp.int32, (8 * pl.cdiv(expert_count, 8), row_count), 0)
    named = (first == ids) | (second == ids)
    above = lax.broadcasted_iota(jnp.int32, (row_count, row_count), 0)
    below = lax.broadcasted_iota(jnp.int32, (row_count, row_count), 1)
    strict = (above < below).astype(F32).astype(BF16)
    earlier = jnp.dot(named.astype(F32).astype(BF16), strict, preferred_element_type=F32)
    return jnp.where(named, earlier.astype(jnp.int32), -1), ids


def dispatch_kernel(me_ref, routes_ref, tokens_ref, *out_refs):
    capacity = out_refs[0].shape[0]
    slots, ids = slots_of(routes_ref, len(out_refs))
    tokens = tokens_ref[...]
    slot_ids = lax.broadcasted_iota(jnp.int32, (capacity, tokens.shape[0]), 0)
    for j in range(len(out_refs)):
        mine = jnp.max(jnp.where(ids == me_ref[0] ^ j, slots, -1), axis=0, keepdims=True)
        placement = (slot_ids == mine).astype(F32).astype(BF16)
        out_refs[j][...] = jnp.dot(placement, tokens, preferred_element_type=F32).astype(BF16)


def mixing_kernel(me_ref, routes_ref, scores_ref, *out_refs):
    row_count, capacity = out_refs[0].shape
    slots, ids = slots_of(routes_ref, len(out_refs))
    scores = scores_ref[...].astype(F32)
    weights = scores / jnp.sum(scores, axis=0, keepdims=True)
    slot_ids = lax.broadcasted_iota(jnp.int32, (capacity, row_count), 0)
    for j in range(len(out_refs)):
        expert = me_ref[0] ^ j
        mine = jnp.max(jnp.where(ids == expert, slots, -1), axis=0, keepdims=True)
        weight = jnp.where(routes_ref[0:1, :] == expert, weights[0:1, :], weights[1:2, :])
        out_refs[j][...] = jnp.where(slot_ids == mine, weight, 0.0).T.astype(BF16)


def mixing(me, routes, scores, expert_count, capacity, deps=()):
    return call(
        mixing_kernel,
        "mixing",
        [(routes.shape[0], capacity)] * expert_count,
        [me, routes.T, scores.T],
        deps,
        specs=[SMEM, VMEM, VMEM],
    )


def combine_kernel(*refs):
    ins, out_ref = refs[:-1], refs[-1]
    total = ins[-1][...] if len(ins) % 2 else None
    for mix_ref, rows_ref in zip(ins[0:-1:2], ins[1::2]):
        part = jnp.dot(mix_ref[...], rows_ref[...], preferred_element_type=F32)
        total = part if total is None else total + part
    out_ref[...] = total.astype(out_ref.dtype)


def expert_kernel(me_ref, mine_ref, theirs_ref, gate_ref, up_ref, down_ref, keep_ref, *rest):
    me = me_ref[1]
    give_refs, hidden = rest[:-1], rest[-1]
    chips, _, width = mine_ref.shape
    units = hidden.shape[1]
    slots = [(ref, j, me ^ (2 * j + core)) for core, ref in enumerate((mine_ref, theirs_ref)) for j in range(chips)]
    for start in range(0, units, width):
        columns = slice(start, start + width)
        gate = up = None
        for ref, j, source in slots:
            rows = pl.ds(pl.multiple_of(source * width, width), width)
            x = ref[j]
            g = jnp.dot(x, gate_ref[rows, columns], preferred_element_type=F32)
            u = jnp.dot(x, up_ref[rows, columns], preferred_element_type=F32)
            gate = g if gate is None else gate + g
            up = u if up is None else up + u
        hidden[:, columns] = (gate / (1.0 + jnp.exp(-gate)) * up).astype(BF16)
    slots = [(ref, me ^ (2 * j + 1)) for j, ref in enumerate(give_refs)]
    slots += [(keep_ref.at[j], me ^ (2 * j)) for j in range(chips)]
    for ref, target in slots:
        columns = pl.ds(pl.multiple_of(target * width, width), width)
        ref[...] = jnp.dot(hidden[...], down_ref[:, columns], preferred_element_type=F32).astype(BF16)


def hub(name, outputs, deps=()):
    arrays = []
    for _, entries in outputs:
        for _, terms in entries:
            arrays += [array for array, _ in terms if not any(array is seen for seen in arrays)]
    position = {id(array): i for i, array in enumerate(arrays)}

    def body(*refs):
        for out_ref, (_, entries) in zip(refs[len(arrays) :], outputs):
            for place, terms in entries:
                values = [refs[position[id(array)]][at] for array, at in terms]
                if len(values) == 1:
                    out_ref[place] = values[0]
                else:
                    out_ref[place] = sum(v.astype(F32) for v in values).astype(BF16)

    return call(body, name, [shape for shape, _ in outputs], arrays, deps)


def load_kernel(gate_ref, up_ref, down_ref, new_gate_ref, new_up_ref, new_down_ref, sems):
    pairs = ((gate_ref, new_gate_ref), (up_ref, new_up_ref), (down_ref, new_down_ref))
    copies = [pltpu.make_async_copy(old, new, sems.at[i]) for i, (old, new) in enumerate(pairs)]
    for copy in copies:
        copy.start()
    for copy in copies:
        copy.wait()


def experts_by_chips(outgoing, weights, me, routes, scores):
    capacity, width = outgoing[0].shape
    units = weights[0].shape[1]
    half = capacity // 2
    top, bot = slice(0, half), slice(half, capacity)
    pieces = [outgoing[j] if j == 0 else over_expert(outgoing[j], j) for j in ORDER]
    count = len(pieces)
    from_x, from_y, relay_x, relay_y, sums_x, sums_y, last_x, last_y = ({} for _ in range(8))
    keep, got, mix, back = {}, {}, None, {}

    def both(c, j, rows, extra=()):
        return [(keep[c], (j, rows)), (got[c][j], rows), *extra]

    def send(steps):
        to_x, to_y, lands = [], [], []
        for kind, c in steps:
            at = len(to_x), len(to_y)
            if kind == "piece":
                to_x += [[(pieces[c], top)], [(pieces[c], bot)]]
                to_y += [[(pieces[c], top)], [(pieces[c], bot)]]
            elif kind == "relay":
                to_x += [[from_y[c][0]]]
                to_y += [[from_x[c][1]]]
            elif kind == "diagonal":
                to_x += [both(c, 3, top)]
                to_y += [both(c, 3, bot)]
            else:
                to_x += [both(c, 1, top), both(c, 1, bot, sums_y[c])]
                to_y += [both(c, 2, top, sums_x[c]), both(c, 2, bot)]
            lands.append((kind, c, *at, len(to_x)))
        return to_x, to_y, lands

    def land(lands, got_x, got_y):
        kinds = {
            "piece": (from_x, from_y),
            "relay": (relay_x, relay_y),
            "diagonal": (sums_x, sums_y),
            "near": (last_x, last_y),
        }
        for kind, c, at_x, at_y, end in lands:
            for store, array, at in zip(kinds[kind], (got_x, got_y), (at_x, at_y)):
                store[c] = [(array, i) for i in range(at, at + end - at_x)]

    def phase(name, steps, ready=None, results=(), deps=()):
        to_x, to_y, lands = send(steps)
        outputs = [((len(p), half, width), [(i, terms) for i, terms in enumerate(p)]) for p in (to_x, to_y) if p]
        if ready is not None:
            c = ready
            terms = [(0, top), (0, bot), (1, top), (1, bot), (2, top), (2, bot), (3, top), (3, bot)]
            views = [(pieces[c], top), (pieces[c], bot), *from_x[c], *from_y[c], *relay_x[c], *relay_y[c]]
            outputs.append(((4, capacity, width), [(place, [view]) for place, view in zip(terms, views)]))
        for c in results:
            rows = [
                (place, [*both(c, 0, place), last_x[c][i], last_y[c][i]]) for i, place in enumerate((top, bot))
            ]
            outputs.append(((capacity, width), rows))
        made = hub(name, outputs, deps)
        rest = made
        if to_x:
            land(lands, over_dp(made[0], X), over_dp(made[1], Y))
            rest = made[2:]
        if ready is not None:
            give_to = over_dp(rest[0], CORE)
            keep[ready], *give = call(
                expert_kernel,
                "expert",
                [(4, capacity, width)] + [(capacity, width)] * 4,
                [me, rest[0], give_to, *matrices],
                specs=[SMEM] + [VMEM] * 5,
                scratch=[pltpu.VMEM((capacity, units), BF16)],
            )
            got[ready] = [over_dp(array, CORE) for array in give]
            rest = rest[1:]
        for c, result in zip(results, rest):
            back[c] = over_expert(result, ORDER[c]) if ORDER[c] else result
        return made[0]

    land([("piece", 0, 0, 0, 2)], over_dp(pieces[0].reshape(2, half, width), X), over_dp(pieces[0].reshape(2, half, width), Y))
    matrices = call(
        load_kernel,
        "load",
        [w.shape for w in weights],
        [pltpu.with_memory_space_constraint(w, pltpu.HBM) for w in weights],
        (outgoing[0],),
        specs=[ANY] * 3,
        scratch=[pltpu.SemaphoreType.DMA((3,))],
    )
    made = phase("hub_b", [("relay", 0), ("piece", 1)], deps=(matrices[0],))
    mix = [mixing(me, routes, scores, count, capacity, (made,))[j] for j in ORDER]
    phase("hub_c", [("relay", 1), ("piece", 2)], ready=0, deps=(mix[0],))
    phase("hub_d", [("relay", 2), ("piece", 3)], ready=1, deps=(keep[0],))
    phase("hub_e", [("relay", 3), ("diagonal", 1)], ready=2)
    phase("hub_f", [("diagonal", 2), ("near", 1)], ready=3)
    phase("hub_g", [("diagonal", 3), ("diagonal", 0), ("near", 2)], results=(1,))
    acc = call(combine_kernel, "combine", [routes.shape[:1] + (width,)], [mix[1], back[1]], dtype=F32)[0]
    phase("hub_h", [("near", 3), ("near", 0)], results=(2,), deps=(acc,))
    acc = call(combine_kernel, "combine", [acc.shape], [mix[2], back[2], acc], dtype=F32)[0]
    phase("hub_i", [], results=(3, 0), deps=(acc,))
    acc = call(combine_kernel, "combine", [acc.shape], [mix[0], back[0], acc], dtype=F32)[0]
    return call(combine_kernel, "combine", [acc.shape], [mix[3], back[3], acc])[0]


def experts_by_axes(outgoing, weights):
    expert_count = lax.axis_size("expert")
    capacity, width = outgoing[0].shape
    me = lax.axis_index("expert")
    order = jnp.arange(expert_count) ^ me
    rows = jnp.stack(outgoing)[order]
    rows = lax.all_to_all(rows, "expert", split_axis=0, concat_axis=0, tiled=True)
    rows = lax.all_gather(rows.reshape(-1, width), "dp", axis=1, tiled=True)
    gate = jnp.dot(rows, weights[0], preferred_element_type=F32)
    up = jnp.dot(rows, weights[1], preferred_element_type=F32)
    hidden = (jax.nn.silu(gate) * up).astype(BF16)
    part = jnp.dot(hidden, weights[2], preferred_element_type=F32).astype(BF16)
    total = lax.psum_scatter(part, "dp", scatter_dimension=1, tiled=True)
    back = lax.all_to_all(
        total.reshape(expert_count, capacity, width), "expert", split_axis=0, concat_axis=0, tiled=True
    )[order]
    return [back[j] for j in range(expert_count)]


def shards(tokens, routes, scores, gate_weight, up_weight, down_weight):
    expert_count = lax.axis_size("expert")
    row_count = tokens.shape[0]
    capacity = 3 * row_count // expert_count
    me = jnp.stack([lax.axis_index("expert"), lax.axis_index("dp")]).astype(jnp.int32)
    weights = gate_weight[0], up_weight[0], down_weight[0]

    shape = (capacity, tokens.shape[1])
    outgoing = call(
        dispatch_kernel,
        "dispatch",
        [shape] * expert_count,
        [me, routes.T, tokens],
        specs=[SMEM, VMEM, VMEM],
    )
    if expert_count == 4 and lax.axis_size("dp") == 8:
        return experts_by_chips(outgoing, weights, me, routes, scores)
    mix = mixing(me, routes, scores, expert_count, capacity)
    results = experts_by_axes(outgoing, weights)
    pairs = [array for pair in zip(mix, results) for array in pair]
    return call(combine_kernel, "combine", [tokens.shape], pairs)[0]


def solution(mesh):
    return jax.shard_map(
        shards,
        mesh=mesh,
        in_specs=(
            P("expert", "dp"),
            P("expert", None),
            P("expert", None),
            P("expert", None, "dp"),
            P("expert", None, "dp"),
            P("expert", "dp", None),
        ),
        out_specs=P("expert", "dp"),
        check_vma=False,
    )
```

```python
import functools

import jax
import jax.numpy as jnp
from jax import lax
from jax.experimental import pallas as pl
from jax.experimental.pallas import tpu as pltpu
from jax.sharding import PartitionSpec as P

F32 = jnp.float32
BF16 = jnp.bfloat16
ANY = pl.BlockSpec(memory_space=pl.ANY)
VMEM = pl.BlockSpec(memory_space=pltpu.VMEM)
CORE, X, Y, DIAGONAL = 1, 2, 4, 6
PAD = 16
ORDER = (0, 2, 3, 1)


def over_core(value):
    return lax.ppermute(value, "dp", [(i, i ^ CORE) for i in range(lax.axis_size("dp"))])


def over_links(value, even, odd):
    return lax.ppermute(value, "dp", [(i, i ^ (odd if i & 1 else even)) for i in range(lax.axis_size("dp"))])


def over_expert(value, mask):
    return lax.ppermute(value, "expert", [(i, i ^ mask) for i in range(lax.axis_size("expert"))])


def ordered(body, operand_count, dep_count):
    def kernel(*refs):
        body(*refs[:operand_count], *refs[operand_count + dep_count :])

    return kernel


def call(body, name, shapes, operands, deps=(), specs=None, scratch=(), vmem=16, dtype=BF16):
    return pl.pallas_call(
        ordered(body, len(operands), len(deps)),
        out_shape=[jax.ShapeDtypeStruct(s, dtype) for s in shapes],
        in_specs=(specs or [VMEM] * len(operands)) + [ANY] * len(deps),
        out_specs=[VMEM] * len(shapes),
        scratch_shapes=list(scratch),
        compiler_params=pltpu.CompilerParams(vmem_limit_bytes=vmem << 20),
        cost_estimate=pl.CostEstimate(flops=0, bytes_accessed=0, transcendentals=0),
        name=name,
    )(*operands, *deps)


def slots_of(routes_ref, expert_count):
    row_count = routes_ref.shape[1]
    first, second = routes_ref[0:1, :], routes_ref[1:2, :]
    ids = lax.broadcasted_iota(jnp.int32, (8 * pl.cdiv(expert_count, 8), row_count), 0)
    named = (first == ids) | (second == ids)
    above = lax.broadcasted_iota(jnp.int32, (row_count, row_count), 0)
    below = lax.broadcasted_iota(jnp.int32, (row_count, row_count), 1)
    strict = (above < below).astype(F32).astype(BF16)
    earlier = jnp.dot(named.astype(F32).astype(BF16), strict, preferred_element_type=F32)
    return jnp.where(named, earlier.astype(jnp.int32), -1), ids


def dispatch_kernel(routes_hbm, tokens_hbm, *refs):
    *out_refs, routes_ref, tokens_ref, sems = refs
    loads = [
        pltpu.make_async_copy(routes_hbm, routes_ref, sems.at[0]),
        pltpu.make_async_copy(tokens_hbm, tokens_ref, sems.at[1]),
    ]
    for load in loads:
        load.start()
    capacity = out_refs[0].shape[0]
    me = lax.axis_index("expert")
    loads[0].wait()
    slots, ids = slots_of(routes_ref, len(out_refs))
    slot_ids = lax.broadcasted_iota(jnp.int32, (capacity, tokens_ref.shape[0]), 0)
    loads[1].wait()
    tokens = tokens_ref[...]
    for j in range(len(out_refs)):
        mine = jnp.max(jnp.where(ids == me ^ j, slots, -1), axis=0, keepdims=True)
        placement = (slot_ids == mine).astype(F32).astype(BF16)
        out_refs[j][...] = jnp.dot(placement, tokens, preferred_element_type=F32).astype(BF16)


def mixing_kernel(routes_ref, scores_ref, *out_refs):
    me = lax.axis_index("expert")
    row_count, capacity = out_refs[0].shape
    slots, ids = slots_of(routes_ref, len(out_refs))
    scores = scores_ref[...].astype(F32)
    weights = scores / jnp.sum(scores, axis=0, keepdims=True)
    slot_ids = lax.broadcasted_iota(jnp.int32, (capacity, row_count), 0)
    for j in range(len(out_refs)):
        expert = me ^ j
        mine = jnp.max(jnp.where(ids == expert, slots, -1), axis=0, keepdims=True)
        weight = jnp.where(routes_ref[0:1, :] == expert, weights[0:1, :], weights[1:2, :])
        out_refs[j][...] = jnp.where(slot_ids == mine, weight, 0.0).T.astype(BF16)


def mixing(routes, scores, expert_count, capacity, deps=()):
    return call(
        mixing_kernel,
        "mixing",
        [(routes.shape[0], capacity)] * expert_count,
        [routes.T, scores.T],
        deps,
    )


def combine_kernel(*refs):
    ins, out_ref = refs[:-1], refs[-1]
    total = ins[-1][...] if len(ins) % 2 else None
    for mix_ref, rows_ref in zip(ins[0:-1:2], ins[1::2]):
        part = jnp.dot(mix_ref[...], rows_ref[: mix_ref.shape[1]], preferred_element_type=F32)
        total = part if total is None else total + part
    out_ref[...] = total.astype(out_ref.dtype)


def expert_kernel(mine_ref, theirs_ref, gate_ref, up_ref, down_ref, keep_ref, *rest):
    me = lax.axis_index("dp")
    give_refs, hidden = rest[:-1], rest[-1]
    chips, _, width = mine_ref.shape
    units = hidden.shape[1]
    slots = [(ref, j, me ^ (2 * j + core)) for core, ref in enumerate((mine_ref, theirs_ref)) for j in range(chips)]
    for start in range(0, units, width):
        columns = slice(start, start + width)
        gate = up = None
        for ref, j, source in slots:
            rows = pl.ds(pl.multiple_of(source * width, width), width)
            x = ref[j]
            g = jnp.dot(x, gate_ref[rows, columns], preferred_element_type=F32)
            u = jnp.dot(x, up_ref[rows, columns], preferred_element_type=F32)
            gate = g if gate is None else gate + g
            up = u if up is None else up + u
        hidden[:, columns] = (gate / (1.0 + jnp.exp(-gate)) * up).astype(BF16)
    slots = [(ref, me ^ (2 * j + 1)) for j, ref in enumerate(give_refs)]
    slots += [(keep_ref.at[j], me ^ (2 * j)) for j in range(chips)]
    for ref, target in slots:
        columns = pl.ds(pl.multiple_of(target * width, width), width)
        ref[...] = jnp.dot(hidden[...], down_ref[:, columns], preferred_element_type=F32).astype(BF16)


class Crossed:
    def __init__(self, first, second, axis):
        self.by_core = (first, second) if axis == X else (second, first)


def hub(name, outputs, deps=()):
    arrays = []

    def position(array):
        for i, seen in enumerate(arrays):
            if seen is array:
                return i
        arrays.append(array)
        return len(arrays) - 1

    plans = []
    for core in (0, 1):
        plan = []
        for number, (_, *entries) in enumerate(outputs):
            for place, terms in entries[core % len(entries)]:
                terms = [(a.by_core[core] if isinstance(a, Crossed) else a, at) for a, at in terms]
                plan.append((number, place, [(position(a), at) for a, at in terms]))
        plans.append(plan)

    def body(*refs):
        def run(plan):
            for number, place, terms in plan:
                values = [refs[i][at] for i, at in terms]
                value = values[0] if len(values) == 1 else sum(v.astype(F32) for v in values).astype(BF16)
                refs[len(arrays) + number][place] = value

        core = lax.axis_index("dp") & 1
        for parity in (0, 1):
            pl.when(core == parity)(functools.partial(run, plans[parity]))

    shapes = [shape for shape, *_ in outputs]
    return call(body, name, shapes, arrays, deps)


def load_kernel(gate_ref, up_ref, down_ref, new_gate_ref, new_up_ref, new_down_ref, sems):
    pairs = ((gate_ref, new_gate_ref), (up_ref, new_up_ref), (down_ref, new_down_ref))
    copies = [pltpu.make_async_copy(old, new, sems.at[i]) for i, (old, new) in enumerate(pairs)]
    for copy in copies:
        copy.start()
    for copy in copies:
        copy.wait()


def experts_by_chips(outgoing, weights, routes, scores):
    capacity, width = outgoing[0].shape
    units = weights[0].shape[1]
    half = capacity // 2
    top, bot = slice(0, half), slice(half, capacity)
    rows_at = top
    pieces = [outgoing[j] if j == 0 else over_expert(outgoing[j], j) for j in ORDER]
    count = len(pieces)
    from_x, from_y, relay_x, relay_y, sums_x, sums_y, last_x, last_y = ({} for _ in range(8))
    keep, got, mix, back = {}, {}, None, {}

    def both(c, j, rows, extra=()):
        return [(keep[c], (j, rows)), (got[c][j], rows), *extra]

    def send(steps):
        to_x, to_y, lands = [], [], []
        for kind, c in steps:
            at = len(to_x), len(to_y)
            if kind == "piece":
                to_x += [[(pieces[c], top)], [(pieces[c], bot)]]
                to_y += [[(pieces[c], top)], [(pieces[c], bot)]]
            elif kind == "relay":
                to_x += [[from_y[c][0]]]
                to_y += [[from_x[c][1]]]
            elif kind == "diagonal":
                to_x += [both(c, 3, top)]
                to_y += [both(c, 3, bot)]
            else:
                to_x += [both(c, 1, top), both(c, 1, bot, sums_y[c])]
                to_y += [both(c, 2, top, sums_x[c]), both(c, 2, bot)]
            lands.append((kind, c, *at, len(to_x)))
        return to_x, to_y, lands

    def land(lands, first, second):
        kinds = {
            "piece": (from_x, from_y),
            "relay": (relay_x, relay_y),
            "diagonal": (sums_x, sums_y),
            "near": (last_x, last_y),
        }
        for kind, c, at_x, at_y, end in lands:
            for store, axis, at in zip(kinds[kind], (X, Y), (at_x, at_y)):
                store[c] = [(Crossed(first, second, axis), (i, rows_at)) for i in range(at, at + end - at_x)]

    def phase(name, *groups, ready=None, results=(), deps=(), pads=()):
        outputs, landings = [], []
        for number, steps in enumerate(groups):
            to_x, to_y, lands = send(steps)
            pad = pads[number] if number < len(pads) else 0
            to_x, to_y = (
                [((i, rows_at), terms) for i, terms in enumerate(p)]
                + [((i, slice(half, half + pad)), [(terms[0][0], (*terms[0][1][:-1], slice(0, pad)))]) for i, terms in enumerate(p) if pad]
                for p in (to_x, to_y)
            )
            shape = (len(lands) and lands[-1][-1], half + pad, width)
            outputs += [(shape, to_x, to_y), (shape, to_y, to_x)]
            landings.append(lands)
        if ready is not None:
            c = ready
            terms = [(0, top), (0, bot), (1, top), (1, bot), (2, top), (2, bot), (3, top), (3, bot)]
            views = [(pieces[c], top), (pieces[c], bot), *from_x[c], *from_y[c], *relay_x[c], *relay_y[c]]
            outputs.append(((4, capacity, width), [(place, [view]) for place, view in zip(terms, views)]))
        for c in results:
            rows = [
                (place, [*both(c, 0, place), last_x[c][i], last_y[c][i]]) for i, place in enumerate((top, bot))
            ]
            pad = PAD if c in (1, 2) else 0
            if pad:
                rows.append((slice(capacity, capacity + pad), [(keep[c], (0, slice(0, pad)))]))
            outputs.append(((capacity + pad, width), rows))
        made = hub(name, outputs, deps)
        rest, came = made, []
        for lands in landings:
            came += [over_links(rest[0], X, Y), over_links(rest[1], Y, X)]
            land(lands, *came[-2:])
            rest = rest[2:]
        if ready is not None:
            keep[ready], *give = call(
                expert_kernel,
                "expert",
                [(4, capacity, width)] + [(capacity, width)] * 4,
                [rest[0], over_core(rest[0]), *matrices],
                scratch=[pltpu.VMEM((capacity, units), BF16)],
            )
            got[ready] = [over_core(array) for array in give]
            rest = rest[1:]
        for c, result in zip(results, rest):
            back[c] = over_expert(result, ORDER[c]) if ORDER[c] else result
        return made[0], came

    own = pieces[0].reshape(2, half, width)
    land([("piece", 0, 0, 0, 2)], over_links(own, X, Y), over_links(own, Y, X))
    matrices = call(
        load_kernel,
        "load",
        [w.shape for w in weights],
        [pltpu.with_memory_space_constraint(w, pltpu.HBM) for w in weights],
        (outgoing[0],),
        specs=[ANY] * 3,
        scratch=[pltpu.SemaphoreType.DMA((3,))],
    )
    made, _ = phase("hub_b", [("relay", 0), ("piece", 1)], deps=(matrices[0],))
    mix = [mixing(routes, scores, count, capacity, (made,))[j] for j in ORDER]
    phase("hub_c", [("relay", 1), ("piece", 2)], ready=0, deps=(mix[0],))
    phase("hub_d", [("relay", 2), ("piece", 3)], ready=1, deps=(keep[0],))
    phase("hub_e", [("relay", 3), ("diagonal", 1), ("diagonal", 0)], ready=2)
    phase("hub_f", [("diagonal", 2), ("near", 1)], ready=3)
    phase("hub_g", [("diagonal", 3)], [("near", 2)], results=(1,))
    made, _ = phase("hub_h", [("near", 3)])
    phase("hub_i", [("near", 0)], results=(2,), deps=(made,))
    phase("hub_j", results=(3,), deps=(back[1],))
    phase("hub_k", results=(0,))
    pairs = [array for c in range(count) for array in (mix[c], back[c])]
    return call(combine_kernel, "combine", [(routes.shape[0], width)], pairs)[0]


def experts_by_axes(outgoing, weights):
    expert_count = lax.axis_size("expert")
    capacity, width = outgoing[0].shape
    me = lax.axis_index("expert")
    order = jnp.arange(expert_count) ^ me
    rows = jnp.stack(outgoing)[order]
    rows = lax.all_to_all(rows, "expert", split_axis=0, concat_axis=0, tiled=True)
    rows = lax.all_gather(rows.reshape(-1, width), "dp", axis=1, tiled=True)
    gate = jnp.dot(rows, weights[0], preferred_element_type=F32)
    up = jnp.dot(rows, weights[1], preferred_element_type=F32)
    hidden = (jax.nn.silu(gate) * up).astype(BF16)
    part = jnp.dot(hidden, weights[2], preferred_element_type=F32).astype(BF16)
    total = lax.psum_scatter(part, "dp", scatter_dimension=1, tiled=True)
    back = lax.all_to_all(
        total.reshape(expert_count, capacity, width), "expert", split_axis=0, concat_axis=0, tiled=True
    )[order]
    return [back[j] for j in range(expert_count)]


def shards(tokens, routes, scores, gate_weight, up_weight, down_weight):
    expert_count = lax.axis_size("expert")
    row_count = tokens.shape[0]
    capacity = 3 * row_count // expert_count
    weights = gate_weight[0], up_weight[0], down_weight[0]

    by_chips = expert_count == 4 and lax.axis_size("dp") == 8
    outgoing = call(
        dispatch_kernel,
        "dispatch",
        [(capacity, tokens.shape[1])] * expert_count,
        [pltpu.with_memory_space_constraint(a, pltpu.HBM) for a in (routes.T, tokens)],
        specs=[ANY, ANY],
        scratch=[pltpu.VMEM(routes.shape[::-1], routes.dtype), pltpu.VMEM(tokens.shape, BF16), pltpu.SemaphoreType.DMA((2,))],
    )
    if by_chips:
        return experts_by_chips(outgoing, weights, routes, scores)
    mix = mixing(routes, scores, expert_count, capacity)
    results = experts_by_axes(outgoing, weights)
    pairs = [array for pair in zip(mix, results) for array in pair]
    return call(combine_kernel, "combine", [tokens.shape], pairs)[0]


def solution(mesh):
    return jax.shard_map(
        shards,
        mesh=mesh,
        in_specs=(
            P("expert", "dp"),
            P("expert", None),
            P("expert", None),
            P("expert", None, "dp"),
            P("expert", None, "dp"),
            P("expert", "dp", None),
        ),
        out_specs=P("expert", "dp"),
        check_vma=False,
    )
```

```python
import functools

import jax
import jax.numpy as jnp
from jax import lax
from jax.experimental import pallas as pl
from jax.experimental.pallas import tpu as pltpu
from jax.sharding import PartitionSpec as P

F32 = jnp.float32
BF16 = jnp.bfloat16
ANY = pl.BlockSpec(memory_space=pl.ANY)
VMEM = pl.BlockSpec(memory_space=pltpu.VMEM)
CORE, X, Y, DIAGONAL = 1, 2, 4, 6
PAD = 16
ORDER = (0, 2, 3, 1)


def over_core(value):
    return lax.ppermute(value, "dp", [(i, i ^ CORE) for i in range(lax.axis_size("dp"))])


def over_links(value, even, odd):
    return lax.ppermute(value, "dp", [(i, i ^ (odd if i & 1 else even)) for i in range(lax.axis_size("dp"))])


def over_expert(value, mask):
    return lax.ppermute(value, "expert", [(i, i ^ mask) for i in range(lax.axis_size("expert"))])


def ordered(body, operand_count, dep_count):
    def kernel(*refs):
        body(*refs[:operand_count], *refs[operand_count + dep_count :])

    return kernel


def call(body, name, shapes, operands, deps=(), specs=None, scratch=(), vmem=16, dtype=BF16):
    return pl.pallas_call(
        ordered(body, len(operands), len(deps)),
        out_shape=[jax.ShapeDtypeStruct(s, dtype) for s in shapes],
        in_specs=(specs or [VMEM] * len(operands)) + [ANY] * len(deps),
        out_specs=[VMEM] * len(shapes),
        scratch_shapes=list(scratch),
        compiler_params=pltpu.CompilerParams(vmem_limit_bytes=vmem << 20),
        cost_estimate=pl.CostEstimate(flops=0, bytes_accessed=0, transcendentals=0),
        name=name,
    )(*operands, *deps)


def slots_of(routes_ref, expert_count):
    row_count = routes_ref.shape[1]
    first, second = routes_ref[0:1, :], routes_ref[1:2, :]
    ids = lax.broadcasted_iota(jnp.int32, (8 * pl.cdiv(expert_count, 8), row_count), 0)
    named = (first == ids) | (second == ids)
    above = lax.broadcasted_iota(jnp.int32, (row_count, row_count), 0)
    below = lax.broadcasted_iota(jnp.int32, (row_count, row_count), 1)
    strict = (above < below).astype(F32).astype(BF16)
    earlier = jnp.dot(named.astype(F32).astype(BF16), strict, preferred_element_type=F32)
    return jnp.where(named, earlier.astype(jnp.int32), -1), ids


def dispatch_kernel(routes_hbm, tokens_hbm, *refs):
    *out_refs, routes_ref, tokens_ref, sems = refs
    loads = [
        pltpu.make_async_copy(routes_hbm, routes_ref, sems.at[0]),
        pltpu.make_async_copy(tokens_hbm, tokens_ref, sems.at[1]),
    ]
    for load in loads:
        load.start()
    capacity = out_refs[0].shape[0]
    me = lax.axis_index("expert")
    loads[0].wait()
    slots, ids = slots_of(routes_ref, len(out_refs))
    slot_ids = lax.broadcasted_iota(jnp.int32, (capacity, tokens_ref.shape[0]), 0)
    loads[1].wait()
    tokens = tokens_ref[...]
    for j in range(len(out_refs)):
        mine = jnp.max(jnp.where(ids == me ^ j, slots, -1), axis=0, keepdims=True)
        placement = (slot_ids == mine).astype(F32).astype(BF16)
        out_refs[j][...] = jnp.dot(placement, tokens, preferred_element_type=F32).astype(BF16)


def mixing_kernel(routes_ref, scores_ref, *out_refs):
    me = lax.axis_index("expert")
    row_count, capacity = out_refs[0].shape
    slots, ids = slots_of(routes_ref, len(out_refs))
    scores = scores_ref[...].astype(F32)
    weights = scores / jnp.sum(scores, axis=0, keepdims=True)
    slot_ids = lax.broadcasted_iota(jnp.int32, (capacity, row_count), 0)
    for j in range(len(out_refs)):
        expert = me ^ j
        mine = jnp.max(jnp.where(ids == expert, slots, -1), axis=0, keepdims=True)
        weight = jnp.where(routes_ref[0:1, :] == expert, weights[0:1, :], weights[1:2, :])
        out_refs[j][...] = jnp.where(slot_ids == mine, weight, 0.0).T.astype(BF16)


def mixing(routes, scores, expert_count, capacity, deps=()):
    return call(
        mixing_kernel,
        "mixing",
        [(routes.shape[0], capacity)] * expert_count,
        [routes.T, scores.T],
        deps,
    )


def combine_kernel(*refs):
    ins, out_ref = refs[:-1], refs[-1]
    total = ins[-1][...] if len(ins) % 2 else None
    for mix_ref, rows_ref in zip(ins[0:-1:2], ins[1::2]):
        part = jnp.dot(mix_ref[...], rows_ref[: mix_ref.shape[1]], preferred_element_type=F32)
        total = part if total is None else total + part
    out_ref[...] = total.astype(out_ref.dtype)


def expert_kernel(mine_ref, theirs_ref, gate_ref, up_ref, down_ref, keep_ref, *rest):
    me = lax.axis_index("dp")
    give_refs, hidden = rest[:-1], rest[-1]
    chips, _, width = mine_ref.shape
    units = hidden.shape[1]
    slots = [(ref, j, me ^ (2 * j + core)) for core, ref in enumerate((mine_ref, theirs_ref)) for j in range(chips)]
    for start in range(0, units, width):
        columns = slice(start, start + width)
        gate = up = None
        for ref, j, source in slots:
            rows = pl.ds(pl.multiple_of(source * width, width), width)
            x = ref[j]
            g = jnp.dot(x, gate_ref[rows, columns], preferred_element_type=F32)
            u = jnp.dot(x, up_ref[rows, columns], preferred_element_type=F32)
            gate = g if gate is None else gate + g
            up = u if up is None else up + u
        hidden[:, columns] = (gate / (1.0 + jnp.exp(-gate)) * up).astype(BF16)
    gives = [give_refs[0]]
    for ref in give_refs[1:]:
        gives += [ref] if len(ref.shape) == 2 else [ref.at[j] for j in range(ref.shape[0])]
    slots = [(ref, me ^ (2 * j + 1)) for ref, j in zip(gives, (3, 0, 1, 2))]
    slots += [(keep_ref.at[j], me ^ (2 * j)) for j in range(chips)]
    for ref, target in slots:
        columns = pl.ds(pl.multiple_of(target * width, width), width)
        ref[...] = jnp.dot(hidden[...], down_ref[:, columns], preferred_element_type=F32).astype(BF16)


class Crossed:
    def __init__(self, first, second, axis):
        self.by_core = (first, second) if axis == X else (second, first)


def hub(name, outputs, deps=()):
    arrays = []

    def position(array):
        for i, seen in enumerate(arrays):
            if seen is array:
                return i
        arrays.append(array)
        return len(arrays) - 1

    plans = []
    for core in (0, 1):
        plan = []
        for number, (_, *entries) in enumerate(outputs):
            for place, terms in entries[core % len(entries)]:
                terms = [(a.by_core[core] if isinstance(a, Crossed) else a, at) for a, at in terms]
                plan.append((number, place, [(position(a), at) for a, at in terms]))
        plans.append(plan)

    def body(*refs):
        def run(plan):
            for number, place, terms in plan:
                values = [refs[i][at] for i, at in terms]
                value = values[0] if len(values) == 1 else sum(v.astype(F32) for v in values).astype(BF16)
                refs[len(arrays) + number][place] = value

        core = lax.axis_index("dp") & 1
        for parity in (0, 1):
            pl.when(core == parity)(functools.partial(run, plans[parity]))

    shapes = [shape for shape, *_ in outputs]
    return call(body, name, shapes, arrays, deps)


def hold_kernel(in_ref, out_ref):
    capacity = in_ref.shape[0]
    out_ref[:capacity] = in_ref[...]
    out_ref[capacity:] = in_ref[: out_ref.shape[0] - capacity]


def load_kernel(gate_ref, up_ref, down_ref, new_gate_ref, new_up_ref, new_down_ref, sems):
    pairs = ((gate_ref, new_gate_ref), (up_ref, new_up_ref), (down_ref, new_down_ref))
    copies = [pltpu.make_async_copy(old, new, sems.at[i]) for i, (old, new) in enumerate(pairs)]
    for copy in copies:
        copy.start()
    for copy in copies:
        copy.wait()


def experts_by_chips(outgoing, weights, routes, scores):
    capacity, width = outgoing[0].shape
    units = weights[0].shape[1]
    half = capacity // 2
    top, bot = slice(0, half), slice(half, capacity)
    rows_at = top
    pieces = [outgoing[j] if j == 0 else over_expert(outgoing[j], j) for j in ORDER]
    count = len(pieces)
    from_x, from_y, relay_x, relay_y, sums_x, sums_y, last_x, last_y = ({} for _ in range(8))
    keep, got, mix, back = {}, {}, None, {}

    def both(c, j, rows, extra=()):
        return [(keep[c], (j, rows)), (got[c][j][0], (*got[c][j][1], rows)), *extra]

    def send(steps):
        to_x, to_y, lands = [], [], []
        for kind, c in steps:
            at = len(to_x), len(to_y)
            if kind == "piece":
                to_x += [[(pieces[c], top)], [(pieces[c], bot)]]
                to_y += [[(pieces[c], top)], [(pieces[c], bot)]]
            elif kind == "relay":
                to_x += [[from_y[c][0]]]
                to_y += [[from_x[c][1]]]
            elif kind == "diagonal":
                to_x += [both(c, 3, top)]
                to_y += [both(c, 3, bot)]
            else:
                to_x += [both(c, 1, top), both(c, 1, bot, sums_y[c])]
                to_y += [both(c, 2, top, sums_x[c]), both(c, 2, bot)]
            lands.append((kind, c, *at, len(to_x)))
        return to_x, to_y, lands

    def land(lands, first, second):
        kinds = {
            "piece": (from_x, from_y),
            "relay": (relay_x, relay_y),
            "diagonal": (sums_x, sums_y),
            "near": (last_x, last_y),
        }
        for kind, c, at_x, at_y, end in lands:
            for store, axis, at in zip(kinds[kind], (X, Y), (at_x, at_y)):
                store[c] = [(Crossed(first, second, axis), (i, rows_at)) for i in range(at, at + end - at_x)]

    def phase(name, *groups, ready=None, results=(), deps=(), pads=()):
        outputs, landings = [], []
        for number, steps in enumerate(groups):
            to_x, to_y, lands = send(steps)
            pad = pads[number] if number < len(pads) else 0
            to_x, to_y = (
                [((i, rows_at), terms) for i, terms in enumerate(p)]
                + [((i, slice(half, half + pad)), [(terms[0][0], (*terms[0][1][:-1], slice(0, pad)))]) for i, terms in enumerate(p) if pad]
                for p in (to_x, to_y)
            )
            shape = (len(lands) and lands[-1][-1], half + pad, width)
            outputs += [(shape, to_x, to_y), (shape, to_y, to_x)]
            landings.append(lands)
        if ready is not None:
            c = ready
            terms = [(0, top), (0, bot), (1, top), (1, bot), (2, top), (2, bot), (3, top), (3, bot)]
            views = [(pieces[c], top), (pieces[c], bot), *from_x[c], *from_y[c], *relay_x[c], *relay_y[c]]
            outputs.append(((4, capacity, width), [(place, [view]) for place, view in zip(terms, views)]))
        for c in results:
            rows = [
                (place, [*both(c, 0, place), last_x[c][i], last_y[c][i]]) for i, place in enumerate((top, bot))
            ]
            pad = (0, 2 * PAD, PAD, 0)[c]
            if pad:
                rows.append((slice(capacity, capacity + pad), [(keep[c], (0, slice(0, pad)))]))
            outputs.append(((capacity + pad, width), rows))
        made = hub(name, outputs, deps)
        rest, came = made, []
        for lands in landings:
            came += [over_links(rest[0], X, Y), over_links(rest[1], Y, X)]
            land(lands, *came[-2:])
            rest = rest[2:]
        if ready is not None:
            keep[ready], *give = call(
                expert_kernel,
                "expert",
                [(4, capacity, width), (capacity, width)] + ([(capacity, width)] * 3 if ready in (2, 3) else [(3, capacity, width)]),
                [rest[0], over_core(rest[0]), *matrices],
                scratch=[pltpu.VMEM((capacity, units), BF16)],
            )
            last, *others = [(over_core(array), ()) for array in give]
            if len(others) == 1:
                others = [(others[0][0], (j,)) for j in range(3)]
            got[ready] = [*others, last]
            rest = rest[1:]
        for c, result in zip(results, rest):
            back[c] = over_expert(result, ORDER[c]) if ORDER[c] else result
        return made[0], came

    own = pieces[0].reshape(2, half, width)
    land([("piece", 0, 0, 0, 2)], over_links(own, X, Y), over_links(own, Y, X))
    matrices = call(
        load_kernel,
        "load",
        [w.shape for w in weights],
        [pltpu.with_memory_space_constraint(w, pltpu.HBM) for w in weights],
        (outgoing[0],),
        specs=[ANY] * 3,
        scratch=[pltpu.SemaphoreType.DMA((3,))],
    )
    held = call(hold_kernel, "hold", [(capacity + PAD, width)], [outgoing[ORDER[2]]], (matrices[0],))[0]
    pieces[2] = over_expert(held, ORDER[2])
    made, _ = phase("hub_b", [("piece", 1)], [("relay", 0)])
    mix = [mixing(routes, scores, count, capacity, (made,))[j] for j in ORDER]
    phase("hub_c", [("relay", 1), ("piece", 2)], ready=0, deps=(mix[0], pieces[3]))
    phase("hub_d", [("relay", 2), ("piece", 3)], ready=1, deps=(keep[0],))
    phase("hub_e", [("relay", 3), ("diagonal", 1), ("diagonal", 0)], ready=2)
    phase("hub_f", [("diagonal", 2), ("near", 1)], ready=3)
    phase("hub_g", [("diagonal", 3)], [("near", 2)], results=(1,))
    made, _ = phase("hub_h", [("near", 3)])
    phase("hub_i", [("near", 0)], results=(2,), deps=(made,))
    phase("hub_j", results=(3,), deps=(back[1],))
    phase("hub_k", results=(0,))
    shape = (routes.shape[0], width)
    acc = call(combine_kernel, "combine", [shape], [mix[0], back[0], mix[1], back[1]], dtype=F32)[0]
    return call(combine_kernel, "combine", [shape], [mix[2], back[2], mix[3], back[3], acc])[0]


def experts_by_axes(outgoing, weights):
    expert_count = lax.axis_size("expert")
    capacity, width = outgoing[0].shape
    me = lax.axis_index("expert")
    order = jnp.arange(expert_count) ^ me
    rows = jnp.stack(outgoing)[order]
    rows = lax.all_to_all(rows, "expert", split_axis=0, concat_axis=0, tiled=True)
    rows = lax.all_gather(rows.reshape(-1, width), "dp", axis=1, tiled=True)
    gate = jnp.dot(rows, weights[0], preferred_element_type=F32)
    up = jnp.dot(rows, weights[1], preferred_element_type=F32)
    hidden = (jax.nn.silu(gate) * up).astype(BF16)
    part = jnp.dot(hidden, weights[2], preferred_element_type=F32).astype(BF16)
    total = lax.psum_scatter(part, "dp", scatter_dimension=1, tiled=True)
    back = lax.all_to_all(
        total.reshape(expert_count, capacity, width), "expert", split_axis=0, concat_axis=0, tiled=True
    )[order]
    return [back[j] for j in range(expert_count)]


def shards(tokens, routes, scores, gate_weight, up_weight, down_weight):
    expert_count = lax.axis_size("expert")
    row_count = tokens.shape[0]
    capacity = 3 * row_count // expert_count
    weights = gate_weight[0], up_weight[0], down_weight[0]

    by_chips = expert_count == 4 and lax.axis_size("dp") == 8
    outgoing = call(
        dispatch_kernel,
        "dispatch",
        [(capacity, tokens.shape[1])] * expert_count,
        [pltpu.with_memory_space_constraint(a, pltpu.HBM) for a in (routes.T, tokens)],
        specs=[ANY, ANY],
        scratch=[pltpu.VMEM(routes.shape[::-1], routes.dtype), pltpu.VMEM(tokens.shape, BF16), pltpu.SemaphoreType.DMA((2,))],
    )
    if by_chips:
        return experts_by_chips(outgoing, weights, routes, scores)
    mix = mixing(routes, scores, expert_count, capacity)
    results = experts_by_axes(outgoing, weights)
    pairs = [array for pair in zip(mix, results) for array in pair]
    return call(combine_kernel, "combine", [tokens.shape], pairs)[0]


def solution(mesh):
    return jax.shard_map(
        shards,
        mesh=mesh,
        in_specs=(
            P("expert", "dp"),
            P("expert", None),
            P("expert", None),
            P("expert", None, "dp"),
            P("expert", None, "dp"),
            P("expert", "dp", None),
        ),
        out_specs=P("expert", "dp"),
        check_vma=False,
    )
```

```python
import functools

import jax
import jax.numpy as jnp
from jax import lax
from jax.experimental import pallas as pl
from jax.experimental.pallas import tpu as pltpu
from jax.sharding import PartitionSpec as P

F32 = jnp.float32
BF16 = jnp.bfloat16
ANY = pl.BlockSpec(memory_space=pl.ANY)
VMEM = pl.BlockSpec(memory_space=pltpu.VMEM)
CORE, X, Y, DIAGONAL = 1, 2, 4, 6
PAD = 16
ORDER = (0, 3, 2, 1)


def over_core(value):
    return lax.ppermute(value, "dp", [(i, i ^ CORE) for i in range(lax.axis_size("dp"))])


def over_links(value, even, odd):
    return lax.ppermute(value, "dp", [(i, i ^ (odd if i & 1 else even)) for i in range(lax.axis_size("dp"))])


def over_expert(value, shift):
    count = lax.axis_size("expert")
    return lax.ppermute(value, "expert", [(i, (i + shift) % count) for i in range(count)])


def ordered(body, operand_count, dep_count):
    def kernel(*refs):
        body(*refs[:operand_count], *refs[operand_count + dep_count :])

    return kernel


def call(body, name, shapes, operands, deps=(), specs=None, scratch=(), vmem=16, dtype=BF16):
    return pl.pallas_call(
        ordered(body, len(operands), len(deps)),
        out_shape=[jax.ShapeDtypeStruct(s, dtype) for s in shapes],
        in_specs=(specs or [VMEM] * len(operands)) + [ANY] * len(deps),
        out_specs=[VMEM] * len(shapes),
        scratch_shapes=list(scratch),
        compiler_params=pltpu.CompilerParams(vmem_limit_bytes=vmem << 20),
        cost_estimate=pl.CostEstimate(flops=0, bytes_accessed=0, transcendentals=0),
        name=name,
    )(*operands, *deps)


def slots_of(routes_ref, expert_count):
    row_count = routes_ref.shape[1]
    first, second = routes_ref[0:1, :], routes_ref[1:2, :]
    ids = lax.broadcasted_iota(jnp.int32, (8 * pl.cdiv(expert_count, 8), row_count), 0)
    named = (first == ids) | (second == ids)
    above = lax.broadcasted_iota(jnp.int32, (row_count, row_count), 0)
    below = lax.broadcasted_iota(jnp.int32, (row_count, row_count), 1)
    strict = (above < below).astype(F32).astype(BF16)
    earlier = jnp.dot(named.astype(F32).astype(BF16), strict, preferred_element_type=F32)
    return jnp.where(named, earlier.astype(jnp.int32), -1), ids


def dispatch_kernel(routes_hbm, tokens_hbm, *refs):
    *out_refs, routes_ref, tokens_ref, sems = refs
    loads = [
        pltpu.make_async_copy(routes_hbm, routes_ref, sems.at[0]),
        pltpu.make_async_copy(tokens_hbm, tokens_ref, sems.at[1]),
    ]
    for load in loads:
        load.start()
    capacity = out_refs[0].shape[0]
    me = lax.axis_index("expert")
    loads[0].wait()
    slots, ids = slots_of(routes_ref, len(out_refs))
    slot_ids = lax.broadcasted_iota(jnp.int32, (capacity, tokens_ref.shape[0]), 0)
    loads[1].wait()
    tokens = tokens_ref[...]
    for j in range(len(out_refs)):
        mine = jnp.max(jnp.where(ids == lax.rem(me + j, len(out_refs)), slots, -1), axis=0, keepdims=True)
        placement = (slot_ids == mine).astype(F32).astype(BF16)
        out_refs[j][...] = jnp.dot(placement, tokens, preferred_element_type=F32).astype(BF16)


def mixing_kernel(routes_ref, scores_ref, *out_refs):
    me = lax.axis_index("expert")
    row_count, capacity = out_refs[0].shape
    slots, ids = slots_of(routes_ref, len(out_refs))
    scores = scores_ref[...].astype(F32)
    weights = scores / jnp.sum(scores, axis=0, keepdims=True)
    slot_ids = lax.broadcasted_iota(jnp.int32, (capacity, row_count), 0)
    for j in range(len(out_refs)):
        expert = lax.rem(me + j, len(out_refs))
        mine = jnp.max(jnp.where(ids == expert, slots, -1), axis=0, keepdims=True)
        weight = jnp.where(routes_ref[0:1, :] == expert, weights[0:1, :], weights[1:2, :])
        out_refs[j][...] = jnp.where(slot_ids == mine, weight, 0.0).T.astype(BF16)


def mixing(routes, scores, expert_count, capacity, deps=()):
    return call(
        mixing_kernel,
        "mixing",
        [(routes.shape[0], capacity)] * expert_count,
        [routes.T, scores.T],
        deps,
    )


def combine_kernel(*refs):
    ins, out_ref = refs[:-1], refs[-1]
    total = ins[-1][...] if len(ins) % 2 else None
    for mix_ref, rows_ref in zip(ins[0:-1:2], ins[1::2]):
        part = jnp.dot(mix_ref[...], rows_ref[: mix_ref.shape[1]], preferred_element_type=F32)
        total = part if total is None else total + part
    out_ref[...] = total.astype(out_ref.dtype)


def expert_kernel(mine_ref, theirs_ref, gate_ref, up_ref, down_ref, keep_ref, *rest):
    me = lax.axis_index("dp")
    give_refs, hidden = rest[:-1], rest[-1]
    chips, _, width = mine_ref.shape
    units = hidden.shape[1]
    slots = [(ref, j, me ^ (2 * j + core)) for core, ref in enumerate((mine_ref, theirs_ref)) for j in range(chips)]
    for start in range(0, units, width):
        columns = slice(start, start + width)
        gate = up = None
        for ref, j, source in slots:
            rows = pl.ds(pl.multiple_of(source * width, width), width)
            x = ref[j]
            g = jnp.dot(x, gate_ref[rows, columns], preferred_element_type=F32)
            u = jnp.dot(x, up_ref[rows, columns], preferred_element_type=F32)
            gate = g if gate is None else gate + g
            up = u if up is None else up + u
        hidden[:, columns] = (gate / (1.0 + jnp.exp(-gate)) * up).astype(BF16)
    gives = [give_refs[0]]
    for ref in give_refs[1:]:
        gives += [ref] if len(ref.shape) == 2 else [ref.at[j] for j in range(ref.shape[0])]
    slots = [(ref, me ^ (2 * j + 1)) for ref, j in zip(gives, (3, 0, 1, 2))]
    slots += [(keep_ref.at[j], me ^ (2 * j)) for j in range(chips)]
    for ref, target in slots:
        columns = pl.ds(pl.multiple_of(target * width, width), width)
        ref[...] = jnp.dot(hidden[...], down_ref[:, columns], preferred_element_type=F32).astype(BF16)


class Crossed:
    def __init__(self, first, second, axis):
        self.by_core = (first, second) if axis == X else (second, first)


def hub(name, outputs, deps=()):
    arrays = []

    def position(array):
        for i, seen in enumerate(arrays):
            if seen is array:
                return i
        arrays.append(array)
        return len(arrays) - 1

    plans = []
    for core in (0, 1):
        plan = []
        for number, (_, *entries) in enumerate(outputs):
            for place, terms in entries[core % len(entries)]:
                terms = [(a.by_core[core] if isinstance(a, Crossed) else a, at) for a, at in terms]
                plan.append((number, place, [(position(a), at) for a, at in terms]))
        plans.append(plan)

    def body(*refs):
        def run(plan):
            for number, place, terms in plan:
                values = [refs[i][at] for i, at in terms]
                value = values[0] if len(values) == 1 else sum(v.astype(F32) for v in values).astype(BF16)
                refs[len(arrays) + number][place] = value

        core = lax.axis_index("dp") & 1
        for parity in (0, 1):
            pl.when(core == parity)(functools.partial(run, plans[parity]))

    shapes = [shape for shape, *_ in outputs]
    return call(body, name, shapes, arrays, deps)


def hold_kernel(in_ref, out_ref):
    capacity = in_ref.shape[0]
    out_ref[:capacity] = in_ref[...]
    out_ref[capacity:] = in_ref[: out_ref.shape[0] - capacity]


def load_kernel(*refs):
    *refs, sems = refs
    count = len(refs) // 2
    copies = [pltpu.make_async_copy(refs[i], refs[count + i], sems.at[i]) for i in range(count)]
    for copy in copies:
        copy.start()
    for copy in copies:
        copy.wait()


def load(weights, deps):
    return call(
        load_kernel,
        "load",
        [w.shape for w in weights],
        [pltpu.with_memory_space_constraint(w, pltpu.HBM) for w in weights],
        deps,
        specs=[ANY] * len(weights),
        scratch=[pltpu.SemaphoreType.DMA((len(weights),))],
    )


def experts_by_chips(outgoing, weights, routes, scores):
    capacity, width = outgoing[0].shape
    units = weights[0].shape[1]
    half = capacity // 2
    top, bot = slice(0, half), slice(half, capacity)
    rows_at = top
    pieces = [outgoing[j] if j == 0 else over_expert(outgoing[j], j) for j in ORDER]
    count = len(pieces)
    from_x, from_y, relay_x, relay_y, sums_x, sums_y, last_x, last_y = ({} for _ in range(8))
    keep, got, mix, back = {}, {}, None, {}

    def both(c, j, rows, extra=()):
        return [(keep[c], (j, rows)), (got[c][j][0], (*got[c][j][1], rows)), *extra]

    def send(steps):
        to_x, to_y, lands = [], [], []
        for kind, c in steps:
            at = len(to_x), len(to_y)
            if kind == "piece":
                to_x += [[(pieces[c], top)], [(pieces[c], bot)]]
                to_y += [[(pieces[c], top)], [(pieces[c], bot)]]
            elif kind == "relay":
                to_x += [[from_y[c][0]]]
                to_y += [[from_x[c][1]]]
            elif kind == "diagonal":
                to_x += [both(c, 3, top)]
                to_y += [both(c, 3, bot)]
            else:
                to_x += [both(c, 1, top), both(c, 1, bot, sums_y[c])]
                to_y += [both(c, 2, top, sums_x[c]), both(c, 2, bot)]
            lands.append((kind, c, *at, len(to_x)))
        return to_x, to_y, lands

    def land(lands, first, second):
        kinds = {
            "piece": (from_x, from_y),
            "relay": (relay_x, relay_y),
            "diagonal": (sums_x, sums_y),
            "near": (last_x, last_y),
        }
        for kind, c, at_x, at_y, end in lands:
            for store, axis, at in zip(kinds[kind], (X, Y), (at_x, at_y)):
                store[c] = [(Crossed(first, second, axis), (i, rows_at)) for i in range(at, at + end - at_x)]

    def phase(name, *groups, ready=None, results=(), deps=(), pads=()):
        outputs, landings = [], []
        for number, steps in enumerate(groups):
            to_x, to_y, lands = send(steps)
            pad = pads[number] if number < len(pads) else 0
            to_x, to_y = (
                [((i, rows_at), terms) for i, terms in enumerate(p)]
                + [((i, slice(half, half + pad)), [(terms[0][0], (*terms[0][1][:-1], slice(0, pad)))]) for i, terms in enumerate(p) if pad]
                for p in (to_x, to_y)
            )
            shape = (len(lands) and lands[-1][-1], half + pad, width)
            outputs += [(shape, to_x, to_y), (shape, to_y, to_x)]
            landings.append(lands)
        if ready is not None:
            c = ready
            terms = [(0, top), (0, bot), (1, top), (1, bot), (2, top), (2, bot), (3, top), (3, bot)]
            views = [(pieces[c], top), (pieces[c], bot), *from_x[c], *from_y[c], *relay_x[c], *relay_y[c]]
            outputs.append(((4, capacity, width), [(place, [view]) for place, view in zip(terms, views)]))
        for c in results:
            rows = [
                (place, [*both(c, 0, place), last_x[c][i], last_y[c][i]]) for i, place in enumerate((top, bot))
            ]
            pad = (0, PAD, PAD, 0)[c]
            if pad:
                rows.append((slice(capacity, capacity + pad), [(keep[c], (0, slice(0, pad)))]))
            outputs.append(((capacity + pad, width), rows))
        made = hub(name, outputs, deps)
        rest, came = made, []
        for lands in landings:
            came += [over_links(rest[0], X, Y), over_links(rest[1], Y, X)]
            land(lands, *came[-2:])
            rest = rest[2:]
        if ready is not None:
            keep[ready], *give = call(
                expert_kernel,
                "expert",
                [(4, capacity, width), (capacity, width)] + ([(capacity, width)] * 3 if ready in (2, 3) else [(3, capacity, width)]),
                [rest[0], over_core(rest[0]), *matrices],
                scratch=[pltpu.VMEM((capacity, units), BF16)],
            )
            last, *others = [(over_core(array), ()) for array in give]
            if len(others) == 1:
                others = [(others[0][0], (j,)) for j in range(3)]
            got[ready] = [*others, last]
            rest = rest[1:]
        for c, result in zip(results, rest):
            back[c] = over_expert(result, -ORDER[c]) if ORDER[c] else result
        return made[0], came

    own = pieces[0].reshape(2, half, width)
    land([("piece", 0, 0, 0, 2)], over_links(own, X, Y), over_links(own, Y, X))
    matrices = load(weights[:2], (outgoing[0],))
    held = call(hold_kernel, "hold", [(capacity + PAD, width)], [outgoing[ORDER[2]]])[0]
    pieces[2] = over_expert(held, ORDER[2])
    made, _ = phase("hub_b", [("piece", 1)], [("relay", 0)], deps=(matrices[0],))
    matrices += load(weights[2:], (made,))
    mix = [mixing(routes, scores, count, capacity, (made,))[j] for j in ORDER]
    phase("hub_c", [("relay", 1), ("piece", 2)], ready=0, deps=(mix[0], matrices[2]))
    phase("hub_d", [("relay", 2), ("piece", 3)], ready=1, deps=(keep[0],))
    phase("hub_e", [("relay", 3), ("diagonal", 1), ("diagonal", 0)], ready=2)
    phase("hub_f", [("diagonal", 2), ("near", 1)], ready=3)
    phase("hub_g", [("diagonal", 3)], [("near", 2)], results=(1,))
    made, _ = phase("hub_h", [("near", 3)])
    phase("hub_i", [("near", 0)], results=(2,), deps=(made,))
    phase("hub_j", results=(3,), deps=(back[1],))
    phase("hub_k", results=(0,))
    shape = (routes.shape[0], width)
    acc = call(combine_kernel, "combine", [shape], [mix[0], back[0], mix[1], back[1]], dtype=F32)[0]
    return call(combine_kernel, "combine", [shape], [mix[2], back[2], mix[3], back[3], acc])[0]


def experts_by_axes(outgoing, weights):
    expert_count = lax.axis_size("expert")
    capacity, width = outgoing[0].shape
    me = lax.axis_index("expert")
    steps = jnp.arange(expert_count)
    rows = jnp.stack(outgoing)[(steps - me) % expert_count]
    rows = lax.all_to_all(rows, "expert", split_axis=0, concat_axis=0, tiled=True)
    rows = lax.all_gather(rows.reshape(-1, width), "dp", axis=1, tiled=True)
    gate = jnp.dot(rows, weights[0], preferred_element_type=F32)
    up = jnp.dot(rows, weights[1], preferred_element_type=F32)
    hidden = (jax.nn.silu(gate) * up).astype(BF16)
    part = jnp.dot(hidden, weights[2], preferred_element_type=F32).astype(BF16)
    total = lax.psum_scatter(part, "dp", scatter_dimension=1, tiled=True)
    back = lax.all_to_all(
        total.reshape(expert_count, capacity, width), "expert", split_axis=0, concat_axis=0, tiled=True
    )[(steps + me) % expert_count]
    return [back[j] for j in range(expert_count)]


def shards(tokens, routes, scores, gate_weight, up_weight, down_weight):
    expert_count = lax.axis_size("expert")
    row_count = tokens.shape[0]
    capacity = 3 * row_count // expert_count
    weights = gate_weight[0], up_weight[0], down_weight[0]

    by_chips = expert_count == 4 and lax.axis_size("dp") == 8
    outgoing = call(
        dispatch_kernel,
        "dispatch",
        [(capacity, tokens.shape[1])] * expert_count,
        [pltpu.with_memory_space_constraint(a, pltpu.HBM) for a in (routes.T, tokens)],
        specs=[ANY, ANY],
        scratch=[pltpu.VMEM(routes.shape[::-1], routes.dtype), pltpu.VMEM(tokens.shape, BF16), pltpu.SemaphoreType.DMA((2,))],
    )
    if by_chips:
        return experts_by_chips(outgoing, weights, routes, scores)
    mix = mixing(routes, scores, expert_count, capacity)
    results = experts_by_axes(outgoing, weights)
    pairs = [array for pair in zip(mix, results) for array in pair]
    return call(combine_kernel, "combine", [tokens.shape], pairs)[0]


def solution(mesh):
    return jax.shard_map(
        shards,
        mesh=mesh,
        in_specs=(
            P("expert", "dp"),
            P("expert", None),
            P("expert", None),
            P("expert", None, "dp"),
            P("expert", None, "dp"),
            P("expert", "dp", None),
        ),
        out_specs=P("expert", "dp"),
        check_vma=False,
    )
```

```python
import functools

import jax
import jax.numpy as jnp
from jax import lax
from jax.experimental import pallas as pl
from jax.experimental.pallas import tpu as pltpu
from jax.sharding import PartitionSpec as P

F32 = jnp.float32
BF16 = jnp.bfloat16
ANY = pl.BlockSpec(memory_space=pl.ANY)
VMEM = pl.BlockSpec(memory_space=pltpu.VMEM)
CORE, X, Y, DIAGONAL = 1, 2, 4, 6
PAD = 16
ORDER = (0, 3, 2, 1)


def over_core(value):
    return lax.ppermute(value, "dp", [(i, i ^ CORE) for i in range(lax.axis_size("dp"))])


def over_links(value, even, odd):
    return lax.ppermute(value, "dp", [(i, i ^ (odd if i & 1 else even)) for i in range(lax.axis_size("dp"))])


def over_expert(value, shift):
    count = lax.axis_size("expert")
    return lax.ppermute(value, "expert", [(i, (i + shift) % count) for i in range(count)])


def ordered(body, operand_count, dep_count):
    def kernel(*refs):
        body(*refs[:operand_count], *refs[operand_count + dep_count :])

    return kernel


def call(body, name, shapes, operands, deps=(), specs=None, scratch=(), vmem=16, dtype=BF16):
    return pl.pallas_call(
        ordered(body, len(operands), len(deps)),
        out_shape=[jax.ShapeDtypeStruct(s, dtype) for s in shapes],
        in_specs=(specs or [VMEM] * len(operands)) + [ANY] * len(deps),
        out_specs=[VMEM] * len(shapes),
        scratch_shapes=list(scratch),
        compiler_params=pltpu.CompilerParams(vmem_limit_bytes=vmem << 20),
        cost_estimate=pl.CostEstimate(flops=0, bytes_accessed=0, transcendentals=0),
        name=name,
    )(*operands, *deps)


def slots_of(routes_ref, expert_count):
    row_count = routes_ref.shape[1]
    first, second = routes_ref[0:1, :], routes_ref[1:2, :]
    ids = lax.broadcasted_iota(jnp.int32, (8 * pl.cdiv(expert_count, 8), row_count), 0)
    named = (first == ids) | (second == ids)
    above = lax.broadcasted_iota(jnp.int32, (row_count, row_count), 0)
    below = lax.broadcasted_iota(jnp.int32, (row_count, row_count), 1)
    strict = (above < below).astype(F32).astype(BF16)
    earlier = jnp.dot(named.astype(F32).astype(BF16), strict, preferred_element_type=F32)
    return jnp.where(named, earlier.astype(jnp.int32), -1), ids


def dispatch_kernel(routes_hbm, tokens_hbm, *refs):
    *out_refs, routes_ref, tokens_ref, sems = refs
    loads = [
        pltpu.make_async_copy(routes_hbm, routes_ref, sems.at[0]),
        pltpu.make_async_copy(tokens_hbm, tokens_ref, sems.at[1]),
    ]
    for load in loads:
        load.start()
    capacity = out_refs[0].shape[0]
    me = lax.axis_index("expert")
    loads[0].wait()
    slots, ids = slots_of(routes_ref, len(out_refs))
    slot_ids = lax.broadcasted_iota(jnp.int32, (capacity, tokens_ref.shape[0]), 0)
    loads[1].wait()
    tokens = tokens_ref[...]
    for j in range(len(out_refs)):
        mine = jnp.max(jnp.where(ids == lax.rem(me + j, len(out_refs)), slots, -1), axis=0, keepdims=True)
        placement = (slot_ids == mine).astype(F32).astype(BF16)
        out_refs[j][...] = jnp.dot(placement, tokens, preferred_element_type=F32).astype(BF16)


def mixing_kernel(routes_ref, scores_ref, *out_refs):
    me = lax.axis_index("expert")
    row_count, capacity = out_refs[0].shape
    slots, ids = slots_of(routes_ref, len(out_refs))
    scores = scores_ref[...].astype(F32)
    weights = scores / jnp.sum(scores, axis=0, keepdims=True)
    slot_ids = lax.broadcasted_iota(jnp.int32, (capacity, row_count), 0)
    for j in range(len(out_refs)):
        expert = lax.rem(me + j, len(out_refs))
        mine = jnp.max(jnp.where(ids == expert, slots, -1), axis=0, keepdims=True)
        weight = jnp.where(routes_ref[0:1, :] == expert, weights[0:1, :], weights[1:2, :])
        out_refs[j][...] = jnp.where(slot_ids == mine, weight, 0.0).T.astype(BF16)


def mixing(routes, scores, expert_count, capacity, deps=()):
    return call(
        mixing_kernel,
        "mixing",
        [(routes.shape[0], capacity)] * expert_count,
        [routes.T, scores.T],
        deps,
    )


def combine_kernel(*refs):
    ins, out_ref = refs[:-1], refs[-1]
    total = ins[-1][...] if len(ins) % 2 else None
    for mix_ref, rows_ref in zip(ins[0:-1:2], ins[1::2]):
        part = jnp.dot(mix_ref[...], rows_ref[: mix_ref.shape[1]], preferred_element_type=F32)
        total = part if total is None else total + part
    out_ref[...] = total.astype(out_ref.dtype)


def expert_kernel(mine_ref, theirs_ref, gate_ref, up_ref, down_ref, keep_ref, *rest):
    me = lax.axis_index("dp")
    give_refs, hidden = rest[:-1], rest[-1]
    chips, _, width = mine_ref.shape
    units = hidden.shape[1]
    slots = [(ref, j, me ^ (2 * j + core)) for core, ref in enumerate((mine_ref, theirs_ref)) for j in range(chips)]
    for start in range(0, units, width):
        columns = slice(start, start + width)
        gate = up = None
        for ref, j, source in slots:
            rows = pl.ds(pl.multiple_of(source * width, width), width)
            x = ref[j]
            g = jnp.dot(x, gate_ref[rows, columns], preferred_element_type=F32)
            u = jnp.dot(x, up_ref[rows, columns], preferred_element_type=F32)
            gate = g if gate is None else gate + g
            up = u if up is None else up + u
        hidden[:, columns] = (gate / (1.0 + jnp.exp(-gate)) * up).astype(BF16)
    gives = [give_refs[0]]
    for ref in give_refs[1:]:
        gives += [ref] if len(ref.shape) == 2 else [ref.at[j] for j in range(ref.shape[0])]
    slots = [(ref, me ^ (2 * j + 1)) for ref, j in zip(gives, (3, 0, 1, 2))]
    slots += [(keep_ref.at[j], me ^ (2 * j)) for j in range(chips)]
    for ref, target in slots:
        columns = pl.ds(pl.multiple_of(target * width, width), width)
        ref[...] = jnp.dot(hidden[...], down_ref[:, columns], preferred_element_type=F32).astype(BF16)


class Crossed:
    def __init__(self, first, second, axis):
        self.by_core = (first, second) if axis == X else (second, first)


def hub(name, outputs, deps=()):
    arrays = []

    def position(array):
        for i, seen in enumerate(arrays):
            if seen is array:
                return i
        arrays.append(array)
        return len(arrays) - 1

    plans = []
    for core in (0, 1):
        plan = []
        for number, (_, *entries) in enumerate(outputs):
            for place, terms in entries[core % len(entries)]:
                terms = [(a.by_core[core] if isinstance(a, Crossed) else a, at) for a, at in terms]
                plan.append((number, place, [(position(a), at) for a, at in terms]))
        plans.append(plan)

    def body(*refs):
        def run(plan):
            for number, place, terms in plan:
                values = [refs[i][at] for i, at in terms]
                value = values[0] if len(values) == 1 else sum(v.astype(F32) for v in values).astype(BF16)
                refs[len(arrays) + number][place] = value

        core = lax.axis_index("dp") & 1
        for parity in (0, 1):
            pl.when(core == parity)(functools.partial(run, plans[parity]))

    shapes = [shape for shape, *_ in outputs]
    return call(body, name, shapes, arrays, deps)


def hold_kernel(in_ref, out_ref):
    capacity = in_ref.shape[0]
    out_ref[:capacity] = in_ref[...]
    out_ref[capacity:] = in_ref[: out_ref.shape[0] - capacity]


def load_kernel(*refs):
    *refs, sems = refs
    count = len(refs) // 2
    copies = [pltpu.make_async_copy(refs[i], refs[count + i], sems.at[i]) for i in range(count)]
    for copy in copies:
        copy.start()
    for copy in copies:
        copy.wait()


def load(weights, deps):
    return call(
        load_kernel,
        "load",
        [w.shape for w in weights],
        [pltpu.with_memory_space_constraint(w, pltpu.HBM) for w in weights],
        deps,
        specs=[ANY] * len(weights),
        scratch=[pltpu.SemaphoreType.DMA((len(weights),))],
    )


def experts_by_chips(outgoing, weights, routes, scores):
    capacity, width = outgoing[0].shape
    units = weights[0].shape[1]
    half = capacity // 2
    top, bot = slice(0, half), slice(half, capacity)
    rows_at = top
    pieces = [outgoing[j] if j == 0 else over_expert(outgoing[j], j) for j in ORDER]
    count = len(pieces)
    from_x, from_y, relay_x, relay_y, sums_x, sums_y, last_x, last_y = ({} for _ in range(8))
    keep, got, mix, back = {}, {}, None, {}

    def both(c, j, rows, extra=()):
        return [(keep[c], (j, rows)), (got[c][j][0], (*got[c][j][1], rows)), *extra]

    def send(steps):
        to_x, to_y, lands = [], [], []
        for kind, c in steps:
            at = len(to_x), len(to_y)
            if kind == "piece":
                to_x += [[(pieces[c], top)], [(pieces[c], bot)]]
                to_y += [[(pieces[c], top)], [(pieces[c], bot)]]
            elif kind == "relay":
                to_x += [[from_y[c][0]]]
                to_y += [[from_x[c][1]]]
            elif kind == "diagonal":
                to_x += [both(c, 3, top)]
                to_y += [both(c, 3, bot)]
            else:
                to_x += [both(c, 1, top), both(c, 1, bot, sums_y[c])]
                to_y += [both(c, 2, top, sums_x[c]), both(c, 2, bot)]
            lands.append((kind, c, *at, len(to_x)))
        return to_x, to_y, lands

    def land(lands, first, second):
        kinds = {
            "piece": (from_x, from_y),
            "relay": (relay_x, relay_y),
            "diagonal": (sums_x, sums_y),
            "near": (last_x, last_y),
        }
        for kind, c, at_x, at_y, end in lands:
            for store, axis, at in zip(kinds[kind], (X, Y), (at_x, at_y)):
                store[c] = [(Crossed(first, second, axis), (i, rows_at)) for i in range(at, at + end - at_x)]

    def phase(name, *groups, ready=None, results=(), deps=(), pads=()):
        outputs, landings = [], []
        for number, steps in enumerate(groups):
            to_x, to_y, lands = send(steps)
            pad = pads[number] if number < len(pads) else 0
            to_x, to_y = (
                [((i, rows_at), terms) for i, terms in enumerate(p)]
                + [((i, slice(half, half + pad)), [(terms[0][0], (*terms[0][1][:-1], slice(0, pad)))]) for i, terms in enumerate(p) if pad]
                for p in (to_x, to_y)
            )
            shape = (len(lands) and lands[-1][-1], half + pad, width)
            outputs += [(shape, to_x, to_y), (shape, to_y, to_x)]
            landings.append(lands)
        if ready is not None:
            c = ready
            terms = [(0, top), (0, bot), (1, top), (1, bot), (2, top), (2, bot), (3, top), (3, bot)]
            views = [(pieces[c], top), (pieces[c], bot), *from_x[c], *from_y[c], *relay_x[c], *relay_y[c]]
            outputs.append(((4, capacity, width), [(place, [view]) for place, view in zip(terms, views)]))
        for c in results:
            rows = [
                (place, [*both(c, 0, place), last_x[c][i], last_y[c][i]]) for i, place in enumerate((top, bot))
            ]
            pad = (0, PAD, PAD, 0)[c]
            if pad:
                rows.append((slice(capacity, capacity + pad), [(keep[c], (0, slice(0, pad)))]))
            outputs.append(((capacity + pad, width), rows))
        made = hub(name, outputs, deps)
        rest, came = made, []
        for lands in landings:
            came += [over_links(rest[0], X, Y), over_links(rest[1], Y, X)]
            land(lands, *came[-2:])
            rest = rest[2:]
        if ready is not None:
            keep[ready], *give = call(
                expert_kernel,
                "expert",
                [(4, capacity, width), (capacity, width)] + ([(capacity, width)] * 3 if ready in (2, 3) else [(3, capacity, width)]),
                [rest[0], over_core(rest[0]), *matrices],
                scratch=[pltpu.VMEM((capacity, units), BF16)],
            )
            last, *others = [(over_core(array), ()) for array in give]
            if len(others) == 1:
                others = [(others[0][0], (j,)) for j in range(3)]
            got[ready] = [*others, last]
            rest = rest[1:]
        for c, result in zip(results, rest):
            back[c] = over_expert(result, -ORDER[c]) if ORDER[c] else result
        return made[0], came

    own = pieces[0].reshape(2, half, width)
    land([("piece", 0, 0, 0, 2)], over_links(own, X, Y), over_links(own, Y, X))
    matrices = load(weights[:1], (outgoing[0],))
    held = call(hold_kernel, "hold", [(capacity + PAD, width)], [outgoing[ORDER[2]]])[0]
    pieces[2] = over_expert(held, ORDER[2])
    made, _ = phase("hub_b", [("piece", 1)], [("relay", 0)], deps=(matrices[0],))
    matrices += load(weights[1:], (made,))
    phase("hub_c", [("relay", 1), ("piece", 2)], ready=0, deps=(matrices[2],))
    phase("hub_d", [("relay", 2), ("piece", 3)], ready=1, deps=(keep[0],))
    phase("hub_e", [("relay", 3), ("diagonal", 1), ("diagonal", 0)], ready=2)
    phase("hub_f", [("diagonal", 2), ("near", 1)], ready=3)
    phase("hub_g", [("diagonal", 3)], [("near", 2)], results=(1,))
    made, _ = phase("hub_h", [("near", 3)])
    mix = [mixing(routes, scores, count, capacity, (made,))[j] for j in ORDER]
    phase("hub_i", [("near", 0)], results=(2,), deps=(mix[0],))
    phase("hub_j", results=(3,), deps=(back[1],))
    phase("hub_k", results=(0,))
    shape = (routes.shape[0], width)
    acc = call(combine_kernel, "combine", [shape], [mix[0], back[0], mix[1], back[1]], dtype=F32)[0]
    return call(combine_kernel, "combine", [shape], [mix[2], back[2], mix[3], back[3], acc])[0]


def experts_by_axes(outgoing, weights):
    expert_count = lax.axis_size("expert")
    capacity, width = outgoing[0].shape
    me = lax.axis_index("expert")
    steps = jnp.arange(expert_count)
    rows = jnp.stack(outgoing)[(steps - me) % expert_count]
    rows = lax.all_to_all(rows, "expert", split_axis=0, concat_axis=0, tiled=True)
    rows = lax.all_gather(rows.reshape(-1, width), "dp", axis=1, tiled=True)
    gate = jnp.dot(rows, weights[0], preferred_element_type=F32)
    up = jnp.dot(rows, weights[1], preferred_element_type=F32)
    hidden = (jax.nn.silu(gate) * up).astype(BF16)
    part = jnp.dot(hidden, weights[2], preferred_element_type=F32).astype(BF16)
    total = lax.psum_scatter(part, "dp", scatter_dimension=1, tiled=True)
    back = lax.all_to_all(
        total.reshape(expert_count, capacity, width), "expert", split_axis=0, concat_axis=0, tiled=True
    )[(steps + me) % expert_count]
    return [back[j] for j in range(expert_count)]


def shards(tokens, routes, scores, gate_weight, up_weight, down_weight):
    expert_count = lax.axis_size("expert")
    row_count = tokens.shape[0]
    capacity = 3 * row_count // expert_count
    weights = gate_weight[0], up_weight[0], down_weight[0]

    by_chips = expert_count == 4 and lax.axis_size("dp") == 8
    outgoing = call(
        dispatch_kernel,
        "dispatch",
        [(capacity, tokens.shape[1])] * expert_count,
        [pltpu.with_memory_space_constraint(a, pltpu.HBM) for a in (routes.T, tokens)],
        specs=[ANY, ANY],
        scratch=[pltpu.VMEM(routes.shape[::-1], routes.dtype), pltpu.VMEM(tokens.shape, BF16), pltpu.SemaphoreType.DMA((2,))],
    )
    if by_chips:
        return experts_by_chips(outgoing, weights, routes, scores)
    mix = mixing(routes, scores, expert_count, capacity)
    results = experts_by_axes(outgoing, weights)
    pairs = [array for pair in zip(mix, results) for array in pair]
    return call(combine_kernel, "combine", [tokens.shape], pairs)[0]


def solution(mesh):
    return jax.shard_map(
        shards,
        mesh=mesh,
        in_specs=(
            P("expert", "dp"),
            P("expert", None),
            P("expert", None),
            P("expert", None, "dp"),
            P("expert", None, "dp"),
            P("expert", "dp", None),
        ),
        out_specs=P("expert", "dp"),
        check_vma=False,
    )
```
